128 devices in a mesh: wide: 16 (over x, z), narrow: 8 (over y, core).
Axes of the slice: x: 4, y: 4, z: 4, core: 2. Of those that a mesh axis runs over, the one named last changes fastest.
Arguments:
- fine_nodes: float32 [262144, 128], P(('wide', 'narrow')), may hold values from -6 to 6
- fine_edges: float32 [1048576, 128], P(('wide', 'narrow')), may hold values from -6 to 6
- fine_sender: int32 [1048576], P(('wide', 'narrow')), may hold values from 0 to 2815, as said below
- fine_offset: int32 [1048576], P(('wide', 'narrow')), may hold values from 0 to 128, as said below
- fine_send: int32 [128, 8, 96], P(('wide', 'narrow')), may hold values from 0 to 2047
- coarse_edges: float32 [65536, 128], P('wide'), may hold values from -6 to 6
- coarse_sender: int32 [65536], P('wide'), may hold values from 0 to 1279, as said below
- coarse_offset: int32 [65536], P('wide'), may hold values from 0 to 128, as said below
- coarse_send: int32 [16, 4, 64], P('wide'), may hold values from 0 to 1023
- restrict_source: int32 [655360], P(('wide', 'narrow')), may hold values from 0 to 2047
- restrict_offset: int32 [655360], P(('wide', 'narrow')), may hold values from 0 to 128
- restrict_tile: int32 [5120], P(('wide', 'narrow')), may hold values from 0 to 7
- restrict_weight: int32 [655360], P(('wide', 'narrow')), may hold values from 0 to 15
- prolong_index: int32 [3, 262144], P(None, ('wide', 'narrow')), may hold values from 0 to 1023
- prolong_weight: int32 [3, 262144], P(None, ('wide', 'narrow')), may hold values from 0 to 15
- restrict_table: float32 [16], replicated, may hold values from 0.2 to 2
- prolong_table: float32 [16], replicated, may hold values from 0.2 to 2
- edge_w1: float32 [4, 384, 128], replicated, may hold values from -0.3125 to 0.3125
- edge_w2: float32 [4, 128, 128], replicated, may hold values from -0.5 to 0.5
- node_w1: float32 [4, 256, 128], replicated, may hold values from -0.375 to 0.375
- node_w2: float32 [4, 128, 128], replicated, may hold values from -0.5 to 0.5
Outputs:
- fine_out: float32 [262144, 128], P(('wide', 'narrow'))
- coarse_out: float32 [16384, 128], P('wide')
The draws below stay inside these ranges and needn't reach their ends.
Inputs may be any that keep to these rules, and one draw needn't show every extreme that they name: `fine_sender`: values below 2048 name the device's own nodes; value 2048 + k * 96 + j names the j-th row that the neighbour of offset k sends to it; every such row is named by some slot whose offset is below 128. `fine_offset`: the value 128 marks an empty slot. `coarse_sender`: values below 1024 name the owner's own coarse nodes; value 1024 + k * 64 + j names the j-th row that the neighbour of offset k sends to it; every such row is named by some slot whose offset is below 128. `coarse_offset`: the value 128 marks an empty slot. fine_send[s, k, j] is the node of device s (local index) sent as the j-th row to the device at offset k from s. coarse_send[s, k, j] is the coarse node of owner s (local index) sent as the j-th row to the owner at offset k from s. `restrict_source`: local index of a node of the device. `restrict_offset`: the value 128 marks an empty entry. `restrict_tile`: tile among the coarse nodes of the device's wide owner. `prolong_index`: local index among the coarse nodes of the fine node's wide owner.
All inputs are finite; a program needn't handle non-finite values.
Results may differ from the reference program's by a relative error of at most 0.0003.
Values sent between devices are 32-bit elements; how exact they have to be, the bound alone decides.
A program may use at most 128 MiB of HBM per device.

```python
import math
import jax
import jax.numpy as jnp
from jax import lax

LATENT = 128
TILE = 128
NODES_DEV = 2048
HALO_CAP = 96
COARSE_CAP = 64
LEVELS = 16
INTERSECTION = 3
RESTRICT_BLOCKS = 40
COARSE_OWN = 1024
EDGES_DEV = 8192
COARSE_EDGES = 4096
COARSE_TILES = 8
FINE_NODES = 262144
COARSE_NODES = 16384
N_WIDE = 16
N_NARROW = 8
DEVICES = 128


def edge_lists(key, salt_value, own_count, groups, length, halo_count):
    key = jax.random.fold_in(key, salt_value)

    def one_group(group_key):
        perm_key, other_key, offset_key, padding_key = jax.random.split(group_key, 4)
        shuffled = jax.random.permutation(perm_key, length)
        ranking = jnp.argsort(shuffled, stable=True).astype(jnp.int32)
        random_source = jax.random.randint(other_key, (length,), 0, own_count + halo_count)
        sender = jnp.where(ranking < halo_count, own_count + ranking, random_source)
        padding = jax.random.randint(padding_key, (), length // 14, length // 7 + 1)
        random_offset = jax.random.randint(offset_key, (length,), 0, TILE)
        offset = jnp.where(ranking >= length - padding, TILE, random_offset)
        return (sender.astype(jnp.int32), offset.astype(jnp.int32))
    senders, offsets = jax.vmap(one_group)(jax.random.split(key, groups))
    return (senders.reshape(-1), offsets.reshape(-1))


def draw_fine_sender(key, part):
    senders, offsets = edge_lists(key, 11, NODES_DEV, DEVICES, EDGES_DEV, 8 * HALO_CAP)
    return senders


def draw_fine_offset(key, part):
    senders, offsets = edge_lists(key, 11, NODES_DEV, DEVICES, EDGES_DEV, 8 * HALO_CAP)
    return offsets


def draw_coarse_sender(key, part):
    senders, offsets = edge_lists(key, 23, COARSE_OWN, N_WIDE, COARSE_EDGES, 4 * COARSE_CAP)
    return senders


def draw_coarse_offset(key, part):
    senders, offsets = edge_lists(key, 23, COARSE_OWN, N_WIDE, COARSE_EDGES, 4 * COARSE_CAP)
    return offsets


def set_ends(array, key, least, top_value):
    shape = array.shape
    place = [jax.random.randint(jax.random.fold_in(key, axis), (), 0, shape[axis]) for axis in range(len(shape))]
    array = array.at[tuple(place)].set(least)
    longest = shape.index(max(shape))
    place[longest] = (place[longest] + 1) % shape[longest]
    return array.at[tuple(place)].set(top_value)


def block_scale(key, dims, cuts, low, top_value):
    def one(position, blocks):
        heights = jax.random.uniform(jax.random.fold_in(jax.random.fold_in(key, 6), position), (blocks,), jnp.float32, low / len(cuts), top_value / len(cuts))
        return jnp.repeat(jnp.exp(heights), dims[position] // blocks).reshape((-1,) + (1,) * (len(dims) - position - 1))

    gain = one(*cuts[0])
    for cut in cuts[1:]:
        gain = gain * one(*cut)
    return gain


def gaussian(stream_key, extent, scale, reach, cuts=(), kind=jnp.bfloat16):
    loudness = block_scale(stream_key, extent, cuts, -0.22, 0.18) if cuts else 1.0
    values = jax.random.normal(stream_key, extent, jnp.float32) * scale * loudness
    return jnp.minimum(jnp.maximum(values, -reach), reach).astype(kind)


def setup_inputs(seed: int = 0) -> dict:
    streams_of = jax.random.split(jax.random.key(seed), 22)
    fine_nodes = gaussian(streams_of[0], (FINE_NODES, LATENT), 1.0, 6.0, ((0, 128),), jnp.float32)
    fine_edges = gaussian(streams_of[1], (DEVICES * EDGES_DEV, LATENT), 1.0, 6.0, ((0, 128),), jnp.float32)
    fine_sender = draw_fine_sender(jax.random.fold_in(streams_of[21], 71), 0)
    fine_offset = draw_fine_offset(jax.random.fold_in(streams_of[21], 71), 0)
    fine_send = set_ends(jax.random.randint(streams_of[4], (DEVICES, 8, HALO_CAP), 0, NODES_DEV), jax.random.fold_in(streams_of[4], 1), 0, NODES_DEV - 1).astype(jnp.int32)
    coarse_edges = gaussian(streams_of[5], (N_WIDE * COARSE_EDGES, LATENT), 1.0, 6.0, ((0, 16),), jnp.float32)
    coarse_sender = draw_coarse_sender(jax.random.fold_in(streams_of[21], 71), 0)
    coarse_offset = draw_coarse_offset(jax.random.fold_in(streams_of[21], 71), 0)
    coarse_send = set_ends(jax.random.randint(streams_of[8], (N_WIDE, 4, COARSE_CAP), 0, COARSE_OWN), jax.random.fold_in(streams_of[8], 1), 0, COARSE_OWN - 1).astype(jnp.int32)
    restrict_source = set_ends(jax.random.randint(streams_of[9], (DEVICES * RESTRICT_BLOCKS * TILE,), 0, NODES_DEV), jax.random.fold_in(streams_of[9], 1), 0, NODES_DEV - 1).astype(jnp.int32)
    restrict_offset = set_ends(jax.random.randint(streams_of[10], (DEVICES * RESTRICT_BLOCKS * TILE,), 0, TILE + 1), jax.random.fold_in(streams_of[10], 1), 0, TILE).astype(jnp.int32)
    restrict_tile = set_ends(jax.random.randint(streams_of[11], (DEVICES * RESTRICT_BLOCKS,), 0, COARSE_TILES), jax.random.fold_in(streams_of[11], 1), 0, COARSE_TILES - 1).astype(jnp.int32)
    restrict_weight = set_ends(jax.random.randint(streams_of[12], (DEVICES * RESTRICT_BLOCKS * TILE,), 0, LEVELS), jax.random.fold_in(streams_of[12], 1), 0, LEVELS - 1).astype(jnp.int32)
    prolong_index = set_ends(jax.random.randint(streams_of[13], (INTERSECTION, FINE_NODES), 0, COARSE_OWN), jax.random.fold_in(streams_of[13], 1), 0, COARSE_OWN - 1).astype(jnp.int32)
    prolong_weight = set_ends(jax.random.randint(streams_of[14], (INTERSECTION, FINE_NODES), 0, LEVELS), jax.random.fold_in(streams_of[14], 1), 0, LEVELS - 1).astype(jnp.int32)
    restrict_table = jnp.clip(jnp.exp(jax.random.uniform(streams_of[15], (LEVELS,), jnp.float32, math.log(0.2), math.log(2.0))), 0.2, 2.0)
    prolong_table = jnp.clip(jnp.exp(jax.random.uniform(streams_of[16], (LEVELS,), jnp.float32, math.log(0.2), math.log(2.0))), 0.2, 2.0)
    edge_w1 = gaussian(streams_of[17], (4, 3 * LATENT, LATENT), (3 * LATENT) ** -0.5, 0.3125, (), jnp.float32)
    edge_w2 = gaussian(streams_of[18], (4, LATENT, LATENT), LATENT ** -0.5, 0.5, (), jnp.float32)
    node_w1 = gaussian(streams_of[19], (4, 2 * LATENT, LATENT), (2 * LATENT) ** -0.5, 0.375, (), jnp.float32)
    node_w2 = gaussian(streams_of[20], (4, LATENT, LATENT), LATENT ** -0.5, 0.5, (), jnp.float32)
    return {"fine_nodes": fine_nodes, "fine_edges": fine_edges, "fine_sender": fine_sender, "fine_offset": fine_offset, "fine_send": fine_send, "coarse_edges": coarse_edges, "coarse_sender": coarse_sender, "coarse_offset": coarse_offset, "coarse_send": coarse_send, "restrict_source": restrict_source, "restrict_offset": restrict_offset, "restrict_tile": restrict_tile, "restrict_weight": restrict_weight, "prolong_index": prolong_index, "prolong_weight": prolong_weight, "restrict_table": restrict_table, "prolong_table": prolong_table, "edge_w1": edge_w1, "edge_w2": edge_w2, "node_w1": node_w1, "node_w2": node_w2}


highest = lax.Precision.HIGHEST
fine_sides = ((-1, -1), (-1, 0), (-1, 1), (0, -1), (0, 1), (1, -1), (1, 0), (1, 1))
coarse_sides = ((-2, 0), (-1, 0), (1, 0), (2, 0))

def matmul(operand, weights):
    return jnp.dot(operand, weights, precision=highest, preferred_element_type=jnp.float32)

def layer_norm(values):
    center = values - lax.optimization_barrier(jnp.mean(values, axis=-1, keepdims=True))
    spread = lax.optimization_barrier(jnp.mean(center * center, axis=-1, keepdims=True))
    return center * lax.rsqrt(spread + 1e-05)

def lookup(level_index, weight_table):
    levels = jnp.arange(weight_table.shape[0], dtype=jnp.int32)
    return lax.optimization_barrier(jnp.sum((level_index[..., None] == levels).astype(jnp.float32) * weight_table, axis=-1))

def graph_step(receivers, source_rows, edge_rows, sender, offset, edge_in, edge_out, node_in, node_out):
    latent = receivers.shape[1]
    tile_count = receivers.shape[0] // TILE
    per_tile = edge_rows.shape[0] // tile_count
    target = jnp.arange(edge_rows.shape[0], dtype=jnp.int32) // per_tile * TILE + jnp.minimum(offset, TILE - 1)
    hidden = matmul(edge_rows, edge_in[:latent]) + matmul(source_rows[sender], edge_in[latent:2 * latent])
    hidden = hidden + matmul(receivers[target], edge_in[2 * latent:])
    new_edges = edge_rows + layer_norm(matmul(jax.nn.relu(hidden), edge_out))
    onehot = (offset.reshape(tile_count, per_tile)[:, :, None] == jnp.arange(TILE, dtype=jnp.int32)).astype(jnp.float32)
    summed = jnp.einsum('tej,teh->tjh', onehot, new_edges.reshape(tile_count, per_tile, latent), precision=highest)
    summed = summed.reshape(-1, latent)
    node_hidden = matmul(receivers, node_in[:latent]) + matmul(summed, node_in[latent:])
    return (receivers + layer_norm(matmul(jax.nn.relu(node_hidden), node_out)), new_edges)

def restrict_partial(fine_rows, source, offset, tile_id, weight_index, weight_table, tile_count):
    blocks = tile_id.shape[0]
    latent = fine_rows.shape[1]
    picked = fine_rows[source].reshape(blocks, TILE, latent)
    scales = lookup(weight_index, weight_table).reshape(blocks, TILE)
    onehot = (offset.reshape(blocks, TILE)[:, :, None] == jnp.arange(TILE, dtype=jnp.int32)).astype(jnp.float32)
    onehot = onehot * scales[:, :, None]
    contrib = jnp.einsum('bej,beh->bjh', onehot, picked, precision=highest)
    weight_sum = lax.optimization_barrier(jnp.sum(onehot, axis=1))
    select = (tile_id[:, None] == jnp.arange(tile_count, dtype=jnp.int32)).astype(jnp.float32)
    numer = jnp.einsum('bt,bjh->tjh', select, contrib, precision=highest).reshape(-1, latent)
    denom = jnp.einsum('bt,bj->tj', select, weight_sum, precision=highest).reshape(-1)
    return (numer, denom)

def prolong_rows(owner_rows, index_rows, weight_index, weight_table):
    scales = lookup(weight_index, weight_table)
    picked = owner_rows[index_rows]
    return lax.optimization_barrier(jnp.sum(scales[:, :, None] * picked, axis=0)) / lax.optimization_barrier(jnp.sum(scales, axis=0))[:, None]

def pick_rows(group_rows, indices):
    return group_rows[indices]

def shift_grid(values, step_wide, step_narrow):
    rolled = jnp.roll(values, (step_wide, step_narrow), axis=(0, 1))
    wide_from = jnp.arange(values.shape[0], dtype=jnp.int32) - step_wide
    narrow_from = jnp.arange(values.shape[1], dtype=jnp.int32) - step_narrow
    wide_ok = (wide_from >= 0) & (wide_from < values.shape[0])
    narrow_ok = (narrow_from >= 0) & (narrow_from < values.shape[1])
    valid = wide_ok[:, None, None, None] & narrow_ok[None, :, None, None]
    return jnp.where(valid, rolled, jnp.zeros_like(rolled))

def neighbour_rows(grid, send_grid, sides):
    pieces = []
    for index, side in enumerate(sides):
        rows = jax.vmap(jax.vmap(pick_rows))(grid, send_grid[:, :, index])
        pieces.append(shift_grid(rows, side[0], side[1]))
    return jnp.concatenate(pieces, axis=2)

def level_step(node_rows, edge_rows, sender, offset, halo_rows, groups, section_index, weights):
    edge_w1, edge_w2, node_w1, node_w2 = weights
    stacked = node_rows.reshape(groups, -1, node_rows.shape[1])
    edge_stack = edge_rows.reshape(groups, -1, edge_rows.shape[1])
    sender_stack = sender.reshape(groups, -1)
    offset_stack = offset.reshape(groups, -1)

    def device_step(target_dev):
        extended = jnp.concatenate([stacked[target_dev], halo_rows[target_dev]], axis=0)
        return graph_step(stacked[target_dev], extended, edge_stack[target_dev], sender_stack[target_dev], offset_stack[target_dev], edge_w1[section_index], edge_w2[section_index], node_w1[section_index], node_w2[section_index])
    new_nodes, new_edges = lax.map(device_step, jnp.arange(groups, dtype=jnp.int32))
    return (new_nodes.reshape(node_rows.shape), new_edges.reshape(edge_rows.shape))

def fine_halo(node_rows, fine_send):
    grid = node_rows.reshape(N_WIDE, N_NARROW, NODES_DEV, LATENT)
    send_grid = fine_send.reshape(N_WIDE, N_NARROW, 8, HALO_CAP)
    return neighbour_rows(grid, send_grid, fine_sides).reshape(DEVICES, 8 * HALO_CAP, LATENT)

def coarse_halo(node_rows, coarse_send):
    grid = node_rows.reshape(N_WIDE, 1, COARSE_OWN, LATENT)
    send_grid = coarse_send.reshape(N_WIDE, 1, 4, COARSE_CAP)
    return neighbour_rows(grid, send_grid, coarse_sides).reshape(N_WIDE, 4 * COARSE_CAP, LATENT)

def reference(fine_nodes, fine_edges, fine_sender, fine_offset, fine_send, coarse_edges, coarse_sender, coarse_offset, coarse_send, restrict_source, restrict_offset, restrict_tile, restrict_weight, prolong_index, prolong_weight, restrict_table, prolong_table, edge_w1, edge_w2, node_w1, node_w2):
    weights = (edge_w1, edge_w2, node_w1, node_w2)
    first_nodes, first_edges = level_step(fine_nodes, fine_edges, fine_sender, fine_offset, fine_halo(fine_nodes, fine_send), DEVICES, 0, weights)
    stacked = first_nodes.reshape(DEVICES, NODES_DEV, LATENT)
    source_stack = restrict_source.reshape(DEVICES, -1)
    offset_stack = restrict_offset.reshape(DEVICES, -1)
    tile_stack = restrict_tile.reshape(DEVICES, -1)
    level_stack = restrict_weight.reshape(DEVICES, -1)

    def partial_for(device):
        return restrict_partial(stacked[device], source_stack[device], offset_stack[device], tile_stack[device], level_stack[device], restrict_table, COARSE_TILES)
    numer, denom = lax.map(partial_for, jnp.arange(DEVICES, dtype=jnp.int32))
    numer = lax.optimization_barrier(jnp.sum(numer.reshape(N_WIDE, N_NARROW, COARSE_OWN, LATENT), axis=1))
    denom = lax.optimization_barrier(jnp.sum(denom.reshape(N_WIDE, N_NARROW, COARSE_OWN), axis=1))
    coarse = (numer / (1.0 + denom)[:, :, None]).reshape(COARSE_NODES, LATENT)
    coarse, coarse_next = level_step(coarse, coarse_edges, coarse_sender, coarse_offset, coarse_halo(coarse, coarse_send), N_WIDE, 1, weights)
    coarse, unused_edges = level_step(coarse, coarse_next, coarse_sender, coarse_offset, coarse_halo(coarse, coarse_send), N_WIDE, 2, weights)
    coarse_stack = coarse.reshape(N_WIDE, COARSE_OWN, LATENT)
    index_stack = prolong_index.reshape(INTERSECTION, DEVICES, NODES_DEV)
    pweight_stack = prolong_weight.reshape(INTERSECTION, DEVICES, NODES_DEV)

    def prolong_for(device):
        return prolong_rows(coarse_stack[device // N_NARROW], index_stack[:, device], pweight_stack[:, device], prolong_table)
    prolonged = lax.map(prolong_for, jnp.arange(DEVICES, dtype=jnp.int32)).reshape(FINE_NODES, LATENT)
    second_in = first_nodes + prolonged
    final_nodes, final_edges = level_step(second_in, first_edges, fine_sender, fine_offset, fine_halo(second_in, fine_send), DEVICES, 3, weights)
    return (final_nodes, coarse)
```

```python
import functools

import jax
import jax.numpy as jnp
from jax import lax
from jax.experimental import pallas as pl
from jax.experimental.pallas import tpu as pltpu
from jax.sharding import PartitionSpec as P

MESH = pl.DeviceIdType.MESH
f32, bf16, i32 = jnp.float32, jnp.bfloat16, jnp.int32
LANES = 128
FINE_SIDES = ((-1, -1), (-1, 0), (-1, 1), (0, -1), (0, 1), (1, -1), (1, 0), (1, 1))
COARSE_SIDES = (-2, -1, 1, 2)
EDGE_OWN, EDGE_FROM, EDGE_TO, EDGE_OUT, NODE_OWN, NODE_SUM, NODE_OUT = range(7)


def halves(values):
    high = values.astype(bf16)
    return high, (values - high.astype(f32)).astype(bf16)


def wide_halves(values):
    return jnp.concatenate(halves(values), axis=1)


def fold(product):
    return product[:, :LANES] + product[:, LANES:]


def dot(left, right):
    return jnp.dot(left, right, preferred_element_type=f32)


def mm(values, weight):
    return fold(dot(wide_halves(values), weight))


def normed(centered):
    return centered * lax.rsqrt(jnp.mean(centered * centered, axis=-1, keepdims=True) + 1e-05)


def as_columns(row):
    return jnp.broadcast_to(row, (LANES, LANES)).T


def lookup(levels, table):
    found = jnp.zeros(levels.shape, f32)
    for level in range(table.shape[0]):
        found = jnp.where(levels == level, table[level], found)
    return found


def sub_iota(shape):
    return lax.broadcasted_iota(i32, shape, 0)


def lane_iota(shape):
    return lax.broadcasted_iota(i32, shape, 1)


def span(start, size):
    return pl.ds(pl.multiple_of(start, size), size)


def take_rows(index_of, count, table, out, out_start, unroll):
    def one(j, carry):
        out[pl.ds(out_start + j, 1), :] = table[pl.ds(index_of(j), 1), :]
        return carry

    lax.fori_loop(0, count, one, 0, unroll=unroll)


def kernel(
    sizes,
    sender, send, csender, csend, rsource, rtile, rtable, ptable,
    foff, coff, roff, rlevel, pindex, plevel,
    x_in, e_in, ce_in, ew1, ew2, nw1, nw2,
    out, cout,
    x, e, base, table, xc, xv, agg, ga, gb, ohg, ohs, wd,
    r_ew1, r_ew2, r_nw1, r_nw2,
    hout1, hin1, hout2, hin2,
    scale, roh, rsel, picked, contrib, rs_out, rs_in, dd_out, dd_in,
    cx, ce, cbase, ctable1, ctable2, cohg, cohs, chout1, chout2, chin1, chin2, cxc, cxv, cg, cfull,
    amat,
    local_sem, h1s, h1r, h2s, h2r, rss, rsr, dds, ddr, a1s, a1r, a2s, a2r, a3s, a3r,
    c1s, c1r, c2s, c2r,
):
    W, N = sizes
    w, n = lax.axis_index("wide"), lax.axis_index("narrow")
    nodes, slots = x.shape[0], e.shape[0]
    halo = send.shape[2]
    tiles = nodes // LANES
    per_tile = slots // tiles
    unit = per_tile // 2
    cown = cfull.shape[0]
    chalo = csend.shape[2]
    cslots = ce.shape[0]
    blocks = rsource.shape[0] // LANES

    def inside(dw, dn):
        return (w + dw >= 0) & (w + dw < W) & (n + dn >= 0) & (n + dn < N)

    def remote(src, dst, send_sem, recv_sem, where):
        return pltpu.make_async_remote_copy(
            src_ref=src, dst_ref=dst, send_sem=send_sem, recv_sem=recv_sem,
            device_id=where, device_id_type=MESH,
        )

    def peer(d):
        return lax.rem(n + d, N)

    own_edges = cslots * n
    loads = [
        pltpu.make_async_copy(x_in, x, local_sem.at[0]),
        pltpu.make_async_copy(ew1, r_ew1, local_sem.at[1]),
        pltpu.make_async_copy(ew2, r_ew2, local_sem.at[2]),
        pltpu.make_async_copy(nw1, r_nw1, local_sem.at[3]),
        pltpu.make_async_copy(nw2, r_nw2, local_sem.at[4]),
        pltpu.make_async_copy(e_in, e, local_sem.at[5]),
        pltpu.make_async_copy(ce_in.at[span(own_edges, cslots)], ce, local_sem.at[6]),
    ]
    for load in loads:
        load.start()

    barrier = pltpu.get_barrier_semaphore()
    others = [(dw, dn) for dw, dn in FINE_SIDES if dw] + [(-2, 0), (2, 0)]
    for d in range(1, N):
        pl.semaphore_signal(barrier, inc=1, device_id=(w, peer(d)), device_id_type=MESH)
    expected = i32(N - 1)
    for dw, dn in others:
        @pl.when(inside(dw, dn))
        def _():
            pl.semaphore_signal(barrier, inc=1, device_id=(w + dw, n + dn), device_id_type=MESH)
        expected = expected + inside(dw, dn).astype(i32)

    def fine_copy(k, hout, hin, ss, rs, where):
        return remote(hout.at[k], hin.at[k], ss.at[k], rs.at[k], where)

    def fine_start(k, hout, hin, ss, rs):
        dw, dn = FINE_SIDES[k]

        @pl.when(inside(dw, dn))
        def _():
            fine_copy(k, hout, hin, ss, rs, (w + dw, n + dn)).start()

    def fine_arrive(k, hout, hin, ss, rs):
        dw, dn = FINE_SIDES[k]

        @pl.when(inside(-dw, -dn))
        def _():
            fine_copy(k, hout, hin, ss, rs, (w - dw, n - dn)).wait_recv()

        @pl.when(jnp.logical_not(inside(-dw, -dn)))
        def _():
            hin[k] = jnp.zeros(hin.shape[1:], f32)

    def fine_sent(k, hout, hin, ss, rs):
        dw, dn = FINE_SIDES[k]

        @pl.when(inside(dw, dn))
        def _():
            fine_copy(k, hout, hin, ss, rs, (w + dw, n + dn)).wait_send()

    def pick_halo(k, hout):
        take_rows(lambda j: send[0, k, j], halo, x, hout.at[k], 0, 16)

    loads[0].wait()
    for k in range(8):
        pick_halo(k, hout1)
    pl.semaphore_wait(barrier, expected)
    for k in range(8):
        fine_start(k, hout1, hin1, h1s, h1r)

    for load in loads[1:5]:
        load.wait()

    def put_weight(section, place, value):
        high, low = halves(value)
        wide = jnp.concatenate([high, low], axis=1)
        wd[section * 7 + place] = jnp.concatenate([wide, wide], axis=0)

    def center(value):
        return value - jnp.mean(value, axis=1, keepdims=True)

    def prepare(s):
        put_weight(s, EDGE_OWN, r_ew1[s, 0:128, :])
        put_weight(s, EDGE_FROM, r_ew1[s, 128:256, :])
        put_weight(s, EDGE_TO, r_ew1[s, 256:384, :])
        put_weight(s, EDGE_OUT, center(r_ew2[s]))
        put_weight(s, NODE_OWN, r_nw1[s, 0:128, :])
        put_weight(s, NODE_SUM, r_nw1[s, 128:256, :])
        put_weight(s, NODE_OUT, center(r_nw2[s]))

    prepare(0)

    def weight(s, place):
        return wd[s * 7 + place]

    lanes = lane_iota((LANES, LANES))
    rows = sub_iota((LANES, LANES))
    per_block = per_tile // LANES

    def one_hots(t, carry):
        for c in range(per_block):
            row = foff[pl.ds(t * per_block + c, 1), :]
            to = as_columns(jnp.minimum(row, LANES - 1))
            ohg[span(t * per_tile + c * LANES, LANES), :] = (to == lanes).astype(f32).astype(bf16)
            ohs[span(t * LANES, LANES), c * LANES : (c + 1) * LANES] = (
                (rows == row).astype(f32).astype(bf16)
            )
        return carry

    lax.fori_loop(0, tiles, one_hots, 0)

    def fine_own(s):
        def project(b, carry):
            part = span(b * 256, 256)
            wide = wide_halves(x[part, :])
            table[part, :] = fold(dot(wide, weight(s, EDGE_FROM)))
            xc[part, :] = wide_halves(fold(dot(wide, weight(s, EDGE_TO))))
            xv[part, :] = fold(dot(wide, weight(s, NODE_OWN)))
            return carry

        lax.fori_loop(0, nodes // 256, project, 0)

    def fine_base(s):
        def one(t, carry):
            to = xc[span(t * LANES, LANES), :]
            for u in range(2):
                part = span(t * per_tile + u * unit, unit)
                base[part, :] = mm(e[part, :], weight(s, EDGE_OWN)) + fold(dot(ohg[part, :], to))
            return carry

        lax.fori_loop(0, tiles, one, 0)

    def fine_halo_in(s, hout, hin, ss, rs):
        for k in range(8):
            fine_arrive(k, hout, hin, ss, rs)
            table[nodes + k * halo : nodes + (k + 1) * halo, :] = mm(hin[k], weight(s, EDGE_FROM))

    def fine_edges_nodes(s, keep, write):
        def fill(t, u, buffer):
            start = t * per_tile + u * unit
            take_rows(lambda j: sender[start + j], unit, table, buffer, 0, UNROLL)

        def part_sum(t, u, buffer):
            part = span(t * per_tile + u * unit, unit)
            h = jnp.maximum(base[part, :] + buffer[...], 0.0)
            fresh = e[part, :] + normed(mm(h, weight(s, EDGE_OUT)))
            if keep:
                e[part, :] = fresh
            onto = ohs[span(t * LANES, LANES), u * unit : (u + 1) * unit]
            return fold(dot(onto, wide_halves(fresh)))

        fill(0, 0, ga)

        def one(t, carry):
            fill(t, 1, gb)
            total = part_sum(t, 0, ga)
            fill(jnp.minimum(t + 1, tiles - 1), 0, ga)
            agg[span(t * LANES, LANES), :] = total + part_sum(t, 1, gb)
            return carry

        lax.fori_loop(0, tiles, one, 0)

        def node(b, carry):
            part = span(b * 256, 256)
            h = jnp.maximum(xv[part, :] + mm(agg[part, :], weight(s, NODE_SUM)), 0.0)
            write(part, x[part, :] + normed(mm(h, weight(s, NODE_OUT))))
            return carry

        lax.fori_loop(0, nodes // 256, node, 0)

    fine_own(0)
    loads[5].wait()
    fine_base(0)
    fine_halo_in(0, hout1, hin1, h1s, h1r)

    def keep_nodes(part, value):
        x[part, :] = value

    fine_edges_nodes(0, True, keep_nodes)

    scale[...] = lookup(rlevel[...], rtable)

    def restrict_block(b, carry):
        take_rows(lambda j: rsource[b * LANES + j], LANES, x, picked, 0, UNROLL)
        row = roff[pl.ds(b, 1), :]
        hit = rows == row
        roh[:, span(b * LANES, LANES)] = hit.astype(f32).astype(bf16)
        left = wide_halves(jnp.where(hit, scale[pl.ds(b, 1), :], 0.0))
        right = wide_halves(picked[...])
        contrib[b] = fold(dot(left, jnp.concatenate([right, right], axis=0)))
        return carry

    lax.fori_loop(0, blocks, restrict_block, 0)

    def restrict_tile(t):
        def add(b, total):
            return total + contrib[b] * (rtile[b] == t).astype(f32)

        rs_out[t] = lax.fori_loop(0, blocks, add, jnp.zeros((LANES, LANES), f32), unroll=4)

    def share_copy(d, toward):
        return remote(rs_out.at[peer(d)], rs_in.at[d], rss.at[d], rsr.at[d], (w, toward))

    for d in range(1, N):
        restrict_tile(peer(d))
        share_copy(d, peer(d)).start()

    def select_block(b, carry):
        kept = jnp.where(sub_iota((8, LANES)) == rtile[b], scale[pl.ds(b, 1), :], 0.0)
        high = kept.astype(bf16).astype(f32)
        rsel[:, span(b * LANES, LANES)] = jnp.concatenate([high, kept - high], axis=0).astype(bf16)
        return carry

    lax.fori_loop(0, blocks, select_block, 0)
    weights = lax.dot_general(
        rsel[...], roh[...], (((1,), (1,)), ((), ())), preferred_element_type=f32
    )
    weights = weights[0:8] + weights[8:16]
    for t in range(N):
        dd_out[t] = jnp.broadcast_to(weights[t : t + 1], (8, LANES))

    def weight_copy(d, toward):
        return remote(dd_out.at[peer(d)], dd_in.at[d], dds.at[d], ddr.at[d], (w, toward))

    for d in range(1, N):
        weight_copy(d, peer(d)).start()
    restrict_tile(n)

    prepare(1)

    def prolong_block(b, carry):
        part = span(b * LANES, LANES)
        raw = [lookup(plevel[k : k + 1, part], ptable) for k in range(3)]
        total = raw[0] + raw[1] + raw[2]
        places = [as_columns(pindex[k : k + 1, part]) for k in range(3)]
        amounts = [as_columns(r / total) for r in raw]
        for c in range(cown // LANES):
            value = jnp.zeros((LANES, LANES), f32)
            for k in range(3):
                value = value + jnp.where(places[k] == lanes + c * LANES, amounts[k], 0.0)
            high, low = halves(value)
            amat[part, c * LANES : (c + 1) * LANES] = high
            amat[part, cown + c * LANES : cown + (c + 1) * LANES] = low
        return carry

    def prolong_weights(part):
        lax.fori_loop(part * tiles // 4, (part + 1) * tiles // 4, prolong_block, 0)

    crow = n * (cslots // LANES)
    for c in range(cslots // LANES):
        row = coff[pl.ds(crow + c, 1), :]
        cohg[c * LANES : (c + 1) * LANES, :] = (
            (as_columns(jnp.minimum(row, LANES - 1)) == lanes).astype(f32).astype(bf16)
        )
        cohs[:, c * LANES : (c + 1) * LANES] = (rows == row).astype(f32).astype(bf16)
    loads[6].wait()
    prolong_weights(0)

    numer = rs_out[n]
    denom = dd_out[n]
    for d in range(1, N):
        share_copy(d, peer(N - d)).wait_recv()
        weight_copy(d, peer(N - d)).wait_recv()
        numer = numer + rs_in[d]
        denom = denom + dd_in[d]
    cx[...] = numer / (1.0 + as_columns(denom[0:1]))

    own = span(n * LANES, LANES)

    def gather_copy(d, rows_ref, ss, rs, source, toward):
        place = rows_ref.at[span(source * LANES, LANES)]
        return remote(place, place, ss.at[d], rs.at[d], (w, toward))

    def gather_start(rows_ref, ss, rs):
        for d in range(1, N):
            gather_copy(d, rows_ref, ss, rs, n, peer(d)).start()

    def gather_arrive(rows_ref, ss, rs):
        for d in range(1, N):
            gather_copy(d, rows_ref, ss, rs, peer(N - d), peer(N - d)).wait_recv()

    def gather_sent(rows_ref, ss, rs):
        for d in range(1, N):
            gather_copy(d, rows_ref, ss, rs, n, peer(d)).wait_send()

    def coarse_copy(k, chin, chout, ss, rs, toward):
        return remote(chout.at[k], chin.at[k], ss.at[k], rs.at[k], (toward, n))

    def coarse_step(s, ctable, chin, chout, gs, gr, cs, cr, keep, meanwhile):
        wide = wide_halves(cx[...])
        ctable[own, :] = fold(dot(wide, weight(s, EDGE_FROM)))
        gather_start(ctable, gs, gr)
        cxc[...] = wide_halves(fold(dot(wide, weight(s, EDGE_TO))))
        cxv[...] = fold(dot(wide, weight(s, NODE_OWN)))
        cbase[...] = mm(ce[...], weight(s, EDGE_OWN)) + fold(dot(cohg[...], cxc[...]))
        meanwhile[0]()
        gather_arrive(ctable, gs, gr)
        for k, dw in enumerate(COARSE_SIDES):
            take_rows(lambda j: csend[0, k, j], chalo, ctable, chout.at[k], 0, 16)

            @pl.when(inside(dw, 0))
            def _():
                coarse_copy(k, chin, chout, cs, cr, w + dw).start()

        meanwhile[1]()
        for k, dw in enumerate(COARSE_SIDES):
            @pl.when(inside(-dw, 0))
            def _():
                coarse_copy(k, chin, chout, cs, cr, w - dw).wait_recv()
                ctable[cown + k * chalo : cown + (k + 1) * chalo, :] = chin[k]

            @pl.when(jnp.logical_not(inside(-dw, 0)))
            def _():
                ctable[cown + k * chalo : cown + (k + 1) * chalo, :] = jnp.zeros((chalo, LANES), f32)

        take_rows(lambda j: csender[n * cslots + j], cslots, ctable, cg, 0, UNROLL)
        h = jnp.maximum(cbase[...] + cg[...], 0.0)
        fresh = ce[...] + normed(mm(h, weight(s, EDGE_OUT)))
        if keep:
            ce[...] = fresh
        total = fold(dot(cohs[...], wide_halves(fresh)))
        h = jnp.maximum(cxv[...] + mm(total, weight(s, NODE_SUM)), 0.0)
        cx[...] = cx[...] + normed(mm(h, weight(s, NODE_OUT)))

    coarse_step(1, ctable1, chin1, chout1, a1s, a1r, c1s, c1r, True,
                (lambda: prolong_weights(1), lambda: prepare(2)))
    coarse_step(2, ctable2, chin2, chout2, a2s, a2r, c2s, c2r, False,
                (lambda: prolong_weights(2), lambda: prolong_weights(3)))

    cfull[own, :] = cx[...]
    gather_start(cfull, a3s, a3r)
    prepare(3)
    gather_arrive(cfull, a3s, a3r)
    cstore = pltpu.make_async_copy(cfull, cout, local_sem.at[7])
    cstore.start()

    cwide = wide_halves(cfull[...])

    def prolong_rows(b, carry):
        part = span(b * 256, 256)
        total = dot(amat[part, 0:cown], cwide) + dot(amat[part, cown:], cwide)
        x[part, :] = x[part, :] + fold(total)
        return carry

    lax.fori_loop(0, nodes // 256, prolong_rows, 0)

    for k in range(8):
        pick_halo(k, hout2)
        fine_start(k, hout2, hin2, h2s, h2r)
    fine_own(3)
    fine_base(3)
    fine_halo_in(3, hout2, hin2, h2s, h2r)

    def write_nodes(part, value):
        agg[part, :] = value

    fine_edges_nodes(3, False, write_nodes)
    store = pltpu.make_async_copy(agg, out, local_sem.at[0])
    store.start()

    for k in range(8):
        fine_sent(k, hout1, hin1, h1s, h1r)
        fine_sent(k, hout2, hin2, h2s, h2r)
    for d in range(1, N):
        share_copy(d, peer(d)).wait_send()
        weight_copy(d, peer(d)).wait_send()
    gather_sent(ctable1, a1s, a1r)
    gather_sent(ctable2, a2s, a2r)
    gather_sent(cfull, a3s, a3r)
    for k, dw in enumerate(COARSE_SIDES):
        @pl.when(inside(dw, 0))
        def _():
            coarse_copy(k, chin1, chout1, c1s, c1r, w + dw).wait_send()
            coarse_copy(k, chin2, chout2, c2s, c2r, w + dw).wait_send()
    cstore.wait()
    store.wait()


UNROLL = 32


def local(
    W, N,
    fine_nodes, fine_edges, fine_sender, fine_offset, fine_send,
    coarse_edges, coarse_sender, coarse_offset, coarse_send,
    restrict_source, restrict_offset, restrict_tile, restrict_weight,
    prolong_index, prolong_weight, restrict_table, prolong_table,
    edge_w1, edge_w2, node_w1, node_w2,
):
    nodes, slots = fine_nodes.shape[0], fine_edges.shape[0]
    halo, chalo = fine_send.shape[2], coarse_send.shape[2]
    tiles = nodes // LANES
    per_tile = slots // tiles
    cown = N * LANES
    cslots = coarse_edges.shape[0] // N
    blocks = restrict_tile.shape[0]
    smem = pl.BlockSpec(memory_space=pltpu.SMEM)
    vmem = pl.BlockSpec(memory_space=pltpu.VMEM)
    hbm = pl.BlockSpec(memory_space=pl.ANY)

    def F(*shape):
        return pltpu.VMEM(shape, f32)

    def B(*shape):
        return pltpu.VMEM(shape, bf16)

    def D(count):
        return pltpu.SemaphoreType.DMA((count,))

    row = lambda flat: flat.reshape(-1, LANES)
    return pl.pallas_call(
        functools.partial(kernel, (W, N)),
        out_shape=(
            jax.ShapeDtypeStruct((nodes, LANES), f32),
            jax.ShapeDtypeStruct((cown, LANES), f32),
        ),
        in_specs=[smem] * 8 + [vmem] * 6 + [hbm] * 7,
        out_specs=(hbm, hbm),
        scratch_shapes=[
            F(nodes, LANES), F(slots, LANES), F(slots, LANES), F(nodes + 8 * halo, LANES),
            B(nodes, 2 * LANES), F(nodes, LANES), F(nodes, LANES),
            F(per_tile // 2, LANES), F(per_tile // 2, LANES),
            B(slots, LANES), B(nodes, per_tile), B(28, 2 * LANES, 2 * LANES),
            F(*edge_w1.shape), F(*edge_w2.shape), F(*node_w1.shape), F(*node_w2.shape),
            F(8, halo, LANES), F(8, halo, LANES), F(8, halo, LANES), F(8, halo, LANES),
            F(blocks, LANES), B(LANES, blocks * LANES), B(16, blocks * LANES), F(LANES, LANES),
            F(blocks, LANES, LANES), F(N, LANES, LANES), F(N, LANES, LANES),
            F(N, 8, LANES), F(N, 8, LANES),
            F(LANES, LANES), F(cslots, LANES), F(cslots, LANES),
            F(cown + 4 * chalo, LANES), F(cown + 4 * chalo, LANES),
            B(cslots, LANES), B(LANES, cslots), F(4, chalo, LANES), F(4, chalo, LANES), F(4, chalo, LANES), F(4, chalo, LANES),
            B(LANES, 2 * LANES), F(LANES, LANES), F(cslots, LANES), F(cown, LANES),
            B(nodes, 2 * cown),
            D(8), D(8), D(8), D(8), D(8), D(N), D(N), D(N), D(N),
            D(N), D(N), D(N), D(N), D(N), D(N), D(4), D(4), D(4), D(4),
        ],
        compiler_params=pltpu.CompilerParams(
            collective_id=0, has_side_effects=True, vmem_limit_bytes=60 << 20
        ),
        name="graph_window",
    )(
        fine_sender, fine_send, coarse_sender, coarse_send, restrict_source, restrict_tile,
        restrict_table, prolong_table,
        row(fine_offset), row(coarse_offset), row(restrict_offset), row(restrict_weight),
        prolong_index, prolong_weight,
        fine_nodes, fine_edges, coarse_edges, edge_w1, edge_w2, node_w1, node_w2,
    )


def solution(mesh):
    both = ("wide", "narrow")
    placed = (
        P(both, None), P(both, None), P(both), P(both), P(both, None, None),
        P("wide", None), P("wide"), P("wide"), P("wide", None, None),
        P(both), P(both), P(both), P(both), P(None, both), P(None, both),
        P(), P(), P(), P(), P(), P(),
    )
    return jax.shard_map(
        functools.partial(local, mesh.shape["wide"], mesh.shape["narrow"]),
        mesh=mesh,
        in_specs=placed,
        out_specs=(P(both, None), P("wide", None)),
        check_vma=False,
    )
```

```python
import functools

import jax
import jax.numpy as jnp
from jax import lax
from jax.experimental import pallas as pl
from jax.experimental.pallas import tpu as pltpu
from jax.sharding import PartitionSpec as P

MESH = pl.DeviceIdType.MESH
f32, bf16, i32 = jnp.float32, jnp.bfloat16, jnp.int32
LANES = 128
CHUNK = 256
FINE_SIDES = ((-1, -1), (-1, 0), (-1, 1), (0, -1), (0, 1), (1, -1), (1, 0), (1, 1))
COARSE_SIDES = (-2, -1, 1, 2)
EDGE_OWN, EDGE_FROM, EDGE_TO, EDGE_OUT, NODE_OWN, NODE_SUM, NODE_OUT = range(7)


def halves(values):
    high = values.astype(bf16)
    return high, (values - high.astype(f32)).astype(bf16)


def wide_halves(values):
    return jnp.concatenate(halves(values), axis=1)


def fold(product):
    return product[:, :LANES] + product[:, LANES:]


def dot(left, right):
    return jnp.dot(left, right, preferred_element_type=f32)


def mm(values, weight):
    return fold(dot(wide_halves(values), weight))


def normed(centered):
    return centered * lax.rsqrt(jnp.mean(centered * centered, axis=-1, keepdims=True) + 1e-05)


def as_columns(row):
    return jnp.broadcast_to(row, (LANES, LANES)).T


def lookup(levels, table):
    found = jnp.zeros(levels.shape, f32)
    for level in range(table.shape[0]):
        found = jnp.where(levels == level, table[level], found)
    return found


def sub_iota(shape):
    return lax.broadcasted_iota(i32, shape, 0)


def lane_iota(shape):
    return lax.broadcasted_iota(i32, shape, 1)


def span(start, size):
    return pl.ds(pl.multiple_of(start, size), size)


def take_rows(index, start, count, table, out):
    window = index.shape[0] - CHUNK + 1

    def some(b, carry):
        first = pl.multiple_of(b * CHUNK, CHUNK)
        there = out.at[pl.ds(first, CHUNK)]
        for j in range(CHUNK):
            place = index.at[pl.ds(j, window)][start + first]
            there[pl.ds(j, 1), :] = table[pl.ds(place, 1), :]
        return carry

    lax.fori_loop(0, count // CHUNK, some, 0)


def take_lists(lists, table, out):
    count, length = out.shape[0], out.shape[1]

    def one(k, carry):
        there = out.at[k]
        for j in range(length):
            there[pl.ds(j, 1), :] = table[pl.ds(lists[0, k, j], 1), :]
        return carry

    lax.fori_loop(0, count, one, 0)


def place_of():
    return lax.axis_index("wide"), lax.axis_index("narrow")


def remote_copy(src, dst, send_sem, recv_sem, where):
    return pltpu.make_async_remote_copy(
        src_ref=src, dst_ref=dst, send_sem=send_sem, recv_sem=recv_sem,
        device_id=where, device_id_type=MESH,
    )


def greetings():
    barrier = pltpu.get_barrier_semaphore()

    def signal(where):
        pl.semaphore_signal(barrier, inc=1, device_id=where, device_id_type=MESH)

    return signal, lambda count: pl.semaphore_wait(barrier, count)


def kernel(
    sizes,
    sender, send, csender, csend, rsource, rtile, rtable, ptable,
    foff, coff, crow, roff, rlevel, pindex, plevel,
    x_in, e_in, ce_in, ew1, ew2, nw1, nw2,
    out, cout,
    x, e, base, table, xc, xv, agg, ga, gb, ohg, ohs, wd,
    r_ew1, r_ew2, r_nw1, r_nw2,
    hout1, hin1, hout2, hin2,
    scale, roh, rsel, picked, contrib, rs_out, rs_in, dd_out, dd_in,
    cx, ce, cbase, ctable, cohg, cohs, cohh, cpick, chout1, chout2, chin1, chin2, cxc, cxv, cagg, cfull,
    amat,
    local_sem, h1s, h1r, h2s, h2r, rss, rsr, dds, ddr, ags, agr,
    c1s, c1r, c2s, c2r,
):
    W, N = sizes
    w, n = place_of()
    nodes, slots = x.shape[0], e.shape[0]
    halo = send.shape[2]
    tiles = nodes // LANES
    per_tile = slots // tiles
    unit = 4 * per_tile
    cown = cfull.shape[0]
    chalo = csend.shape[2]
    cslots = ce.shape[0]
    blocks = rsource.shape[0] // LANES

    def inside(dw, dn):
        return (w + dw >= 0) & (w + dw < W) & (n + dn >= 0) & (n + dn < N)

    def remote(src, dst, send_sem, recv_sem, where):
        return remote_copy(src, dst, send_sem, recv_sem, where)

    def peer(d):
        return lax.rem(n + d, N)

    loads = [
        pltpu.make_async_copy(x_in, x, local_sem.at[0]),
        pltpu.make_async_copy(ew1, r_ew1, local_sem.at[1]),
        pltpu.make_async_copy(ew2, r_ew2, local_sem.at[2]),
        pltpu.make_async_copy(nw1, r_nw1, local_sem.at[3]),
        pltpu.make_async_copy(nw2, r_nw2, local_sem.at[4]),
        pltpu.make_async_copy(e_in, e, local_sem.at[5]),
        pltpu.make_async_copy(ce_in, ce, local_sem.at[6]),
    ]
    for load in loads:
        load.start()

    signal, wait_for = greetings()
    others = [(dw, dn) for dw, dn in FINE_SIDES if dw] + [(-2, 0), (2, 0)]
    for d in range(1, N):
        signal((w, peer(d)))
    expected = i32(N - 1)
    for dw, dn in others:
        @pl.when(inside(dw, dn))
        def _():
            signal((w + dw, n + dn))
        expected = expected + inside(dw, dn).astype(i32)

    def fine_copy(k, hout, hin, ss, rs, where):
        return remote(hout.at[k], hin.at[k], ss.at[k], rs.at[k], where)

    def fine_start(k, hout, hin, ss, rs):
        dw, dn = FINE_SIDES[k]

        @pl.when(inside(dw, dn))
        def _():
            fine_copy(k, hout, hin, ss, rs, (w + dw, n + dn)).start()

    def fine_arrive(k, hout, hin, ss, rs):
        dw, dn = FINE_SIDES[k]

        @pl.when(inside(-dw, -dn))
        def _():
            fine_copy(k, hout, hin, ss, rs, (w - dw, n - dn)).wait_recv()

        @pl.when(jnp.logical_not(inside(-dw, -dn)))
        def _():
            hin[k] = jnp.zeros(hin.shape[1:], f32)

    def fine_sent(k, hout, hin, ss, rs):
        dw, dn = FINE_SIDES[k]

        @pl.when(inside(dw, dn))
        def _():
            fine_copy(k, hout, hin, ss, rs, (w + dw, n + dn)).wait_send()

    loads[0].wait()
    take_lists(send, x, hout1)
    wait_for(expected)
    for k in range(8):
        fine_start(k, hout1, hin1, h1s, h1r)

    for load in loads[1:5]:
        load.wait()

    def put_weight(section, place, value):
        high, low = halves(value)
        wide = jnp.concatenate([high, low], axis=1)
        wd[section * 7 + place] = jnp.concatenate([wide, wide], axis=0)

    def center(value):
        return value - jnp.mean(value, axis=1, keepdims=True)

    def prepare(s):
        put_weight(s, EDGE_OWN, r_ew1[s, 0:128, :])
        put_weight(s, EDGE_FROM, r_ew1[s, 128:256, :])
        put_weight(s, EDGE_TO, r_ew1[s, 256:384, :])
        put_weight(s, EDGE_OUT, center(r_ew2[s]))
        put_weight(s, NODE_OWN, r_nw1[s, 0:128, :])
        put_weight(s, NODE_SUM, r_nw1[s, 128:256, :])
        put_weight(s, NODE_OUT, center(r_nw2[s]))

    prepare(0)

    def weight(s, place):
        return wd[s * 7 + place]

    lanes = lane_iota((LANES, LANES))
    rows = sub_iota((LANES, LANES))
    per_block = per_tile // LANES

    def one_hots(t, carry):
        for c in range(per_block):
            row = foff[pl.ds(t * per_block + c, 1), :]
            to = as_columns(jnp.minimum(row, LANES - 1))
            ohg[span(t * per_tile + c * LANES, LANES), :] = (to == lanes).astype(f32).astype(bf16)
            ohs[span(t * LANES, LANES), c * LANES : (c + 1) * LANES] = (
                (rows == row).astype(f32).astype(bf16)
            )
        return carry

    lax.fori_loop(0, tiles, one_hots, 0, unroll=4)

    def fine_own(s):
        for b in range(nodes // 1024):
            part = slice(b * 1024, (b + 1) * 1024)
            wide = wide_halves(x[part, :])
            table[part, :] = fold(dot(wide, weight(s, EDGE_FROM)))
            xc[part, :] = wide_halves(fold(dot(wide, weight(s, EDGE_TO))))
            xv[part, :] = fold(dot(wide, weight(s, NODE_OWN)))

    def fine_base_edges(s):
        def one(i, carry):
            part = span(i * unit, unit)
            base[part, :] = mm(e[part, :], weight(s, EDGE_OWN))
            return carry

        lax.fori_loop(0, slots // unit, one, 0)

    def fine_base(s, with_edges):
        def one(i, carry):
            part = span(i * unit, unit)
            own = mm(e[part, :], weight(s, EDGE_OWN)) if with_edges else base[part, :]
            to = []
            for t in range(unit // per_tile):
                here = ohg[span(i * unit + t * per_tile, per_tile), :]
                there = xc[span(i * (unit // 4) + t * LANES, LANES), :]
                to.append(fold(dot(here, there)))
            base[part, :] = own + jnp.concatenate(to, axis=0)
            return carry

        lax.fori_loop(0, slots // unit, one, 0)

    def fine_halo_in(s, hout, hin, ss, rs):
        for k in range(8):
            fine_arrive(k, hout, hin, ss, rs)
        rows_in = jnp.concatenate([hin[k] for k in range(8)], axis=0)
        table[nodes:, :] = mm(rows_in, weight(s, EDGE_FROM))

    def fine_edges_nodes(s, keep, write):
        def some(i, carry):
            part = span(i * unit, unit)
            take_rows(sender, i * unit, unit, table, ga)
            h = jnp.maximum(base[part, :] + ga[...], 0.0)
            fresh = e[part, :] + normed(mm(h, weight(s, EDGE_OUT)))
            if keep:
                e[part, :] = fresh
            wide = wide_halves(fresh)
            for t in range(unit // per_tile):
                q = span(i * (unit // 4) + t * LANES, LANES)
                agg[q, :] = fold(dot(ohs[q, :], wide[t * per_tile : (t + 1) * per_tile]))
            return carry

        lax.fori_loop(0, slots // unit, some, 0)
        for b in range(nodes // 1024):
            part = slice(b * 1024, (b + 1) * 1024)
            h = jnp.maximum(xv[part, :] + mm(agg[part, :], weight(s, NODE_SUM)), 0.0)
            write(part, x[part, :] + normed(mm(h, weight(s, NODE_OUT))))

    fine_own(0)
    loads[5].wait()
    fine_base(0, True)
    fine_halo_in(0, hout1, hin1, h1s, h1r)

    def keep_nodes(part, value):
        x[part, :] = value

    fine_edges_nodes(0, True, keep_nodes)

    scale[...] = lookup(rlevel[...], rtable)

    take_rows(rsource, 0, blocks * LANES, x, picked)

    def restrict_block(b, carry):
        row = roff[pl.ds(b, 1), :]
        hit = rows == row
        roh[:, span(b * LANES, LANES)] = hit.astype(f32).astype(bf16)
        left = wide_halves(jnp.where(hit, scale[pl.ds(b, 1), :], 0.0))
        right = wide_halves(picked[span(b * LANES, LANES), :])
        contrib[b] = fold(dot(left, jnp.concatenate([right, right], axis=0)))
        return carry

    lax.fori_loop(0, blocks, restrict_block, 0, unroll=8)

    def restrict_tile(t):
        def add(b, total):
            return total + contrib[b] * (rtile[b] == t).astype(f32)

        rs_out[t] = lax.fori_loop(0, blocks, add, jnp.zeros((LANES, LANES), f32), unroll=8)

    core, chip = lax.rem(n, 2), lax.div(n, 2)
    pair = n + 1 - 2 * core
    chips = N // 2

    def pair_copy(i, tile):
        return remote(rs_out.at[tile], rs_in.at[i], rss.at[i], rsr.at[i], (w, pair))

    def cross_copy(d, tile, toward):
        slot = chips + d
        return remote(rs_out.at[tile], rs_in.at[slot], rss.at[slot], rsr.at[slot], (w, toward))

    for i in range(chips):
        restrict_tile(2 * i + 1 - core)
        pair_copy(i, 2 * i + 1 - core).start()

    def select_block(b, carry):
        kept = jnp.where(sub_iota((8, LANES)) == rtile[b], scale[pl.ds(b, 1), :], 0.0)
        high = kept.astype(bf16).astype(f32)
        rsel[:, span(b * LANES, LANES)] = jnp.concatenate([high, kept - high], axis=0).astype(bf16)
        return carry

    lax.fori_loop(0, blocks, select_block, 0, unroll=8)
    weights = lax.dot_general(
        rsel[...], roh[...], (((1,), (1,)), ((), ())), preferred_element_type=f32
    )
    weights = weights[0:8] + weights[8:16]
    for t in range(N):
        dd_out[t] = jnp.broadcast_to(weights[t : t + 1], (8, LANES))

    def weight_copy(d, toward):
        return remote(dd_out.at[peer(d)], dd_in.at[d], dds.at[d], ddr.at[d], (w, toward))

    for d in range(1, N):
        weight_copy(d, peer(d)).start()
    for i in range(chips):
        restrict_tile(2 * i + core)
    for d in (2, 1, 3, 0):
        place = lax.rem(chip + d, chips)
        tile = 2 * place + core
        pair_copy(place, tile).wait_recv()
        rs_out[tile] = rs_out[tile] + rs_in[place]
        if d:
            cross_copy(d, tile, peer(2 * d)).start()

    cper_tile = cslots // (cown // LANES)

    def coarse_base_edges(s):
        for i in range(cslots // unit):
            part = slice(i * unit, (i + 1) * unit)
            cbase[part, :] = mm(ce[part, :], weight(s, EDGE_OWN))

    prepare(1)

    def prolong_block(b, carry):
        part = span(b * LANES, LANES)
        raw = [lookup(plevel[k : k + 1, part], ptable) for k in range(3)]
        total = raw[0] + raw[1] + raw[2]
        places = [as_columns(pindex[k : k + 1, part]) for k in range(3)]
        amounts = [as_columns(r / total) for r in raw]
        for c in range(cown // LANES):
            value = jnp.zeros((LANES, LANES), f32)
            for k in range(3):
                value = value + jnp.where(places[k] == lanes + c * LANES, amounts[k], 0.0)
            high, low = halves(value)
            amat[part, c * LANES : (c + 1) * LANES] = high
            amat[part, cown + c * LANES : cown + (c + 1) * LANES] = low
        return carry

    def prolong_weights(part):
        lax.fori_loop(part * tiles // 4, (part + 1) * tiles // 4, prolong_block, 0, unroll=2)

    def coarse_one_hots(t, carry):
        for c in range(cper_tile // LANES):
            block = t * (cper_tile // LANES) + c
            row = coff[pl.ds(block, 1), :]
            part = span(block * LANES, LANES)
            cohg[part, :] = (as_columns(jnp.minimum(row, LANES - 1)) == lanes).astype(f32).astype(bf16)
            cohs[span(t * LANES, LANES), c * LANES : (c + 1) * LANES] = (
                (rows == row).astype(f32).astype(bf16)
            )
            origin = as_columns(crow[pl.ds(block, 1), :]) - cown
            for h in range(4 * chalo // LANES):
                cohh[part, h * LANES : (h + 1) * LANES] = (
                    (origin == lanes + h * LANES).astype(f32).astype(bf16)
                )
        return carry

    lax.fori_loop(0, cown // LANES, coarse_one_hots, 0, unroll=2)
    ctable[cown:, :] = jnp.zeros((4 * chalo, LANES), f32)
    loads[6].wait()
    prolong_weights(0)
    prolong_weights(1)

    own = span(n * LANES, LANES)
    numer = rs_out[n]
    for d in range(1, chips):
        cross_copy(d, n, peer(N - 2 * d)).wait_recv()
        numer = numer + rs_in[chips + d]
    denom = dd_out[n]
    for d in range(1, N):
        weight_copy(d, peer(N - d)).wait_recv()
        denom = denom + dd_in[d]
    cx[own, :] = numer / (1.0 + as_columns(denom[0:1]))

    def gather_copy(slot, tile, toward):
        place = cx.at[span(tile * LANES, LANES)]
        return remote(place, place, ags.at[slot], agr.at[slot], (w, toward))

    for d in (2, 1, 3):
        gather_copy(d, n, peer(2 * d)).start()
    gather_copy(0, n, pair).start()
    prepare(2)
    prepare(3)
    prolong_weights(2)
    fine_base_edges(3)
    coarse_base_edges(1)
    for d in (1, 3, 2):
        tile = peer(N - 2 * d)
        gather_copy(d, tile, tile).wait_recv()
        gather_copy(chips + d, tile, pair).start()
    prolong_weights(3)
    gather_copy(0, pair, pair).wait_recv()
    for d in (1, 3, 2):
        gather_copy(chips + d, lax.rem(pair + N - 2 * d, N), pair).wait_recv()

    def coarse_copy(k, chin, chout, ss, rs, toward):
        return remote(chout.at[k], chin.at[k], ss.at[k], rs.at[k], (toward, n))

    def coarse_step(s, chin, chout, cs, cr, keep):
        take_lists(csend, cx, cpick)
        for k in range(4):
            chout[k] = mm(cpick[k], weight(s, EDGE_FROM))
        for k, dw in enumerate(COARSE_SIDES):
            @pl.when(inside(dw, 0))
            def _():
                coarse_copy(k, chin, chout, cs, cr, w + dw).start()

        wide = wide_halves(cx[...])
        ctable[0:cown, :] = fold(dot(wide, weight(s, EDGE_FROM)))
        cxc[...] = wide_halves(fold(dot(wide, weight(s, EDGE_TO))))
        cxv[...] = fold(dot(wide, weight(s, NODE_OWN)))
        if s != 1:
            coarse_base_edges(s)
        for i, buffer in enumerate((ga, gb)):
            part = slice(i * unit, (i + 1) * unit)
            take_rows(csender, i * unit, unit, ctable, buffer)
            to = []
            for t in range(unit // cper_tile):
                q = i * unit + t * cper_tile
                tile = i * (unit // cper_tile) + t
                here = cohg[q : q + cper_tile, :]
                to.append(fold(dot(here, cxc[tile * LANES : (tile + 1) * LANES, :])))
            buffer[...] = buffer[...] + (cbase[part, :] + jnp.concatenate(to, axis=0))
        for k, dw in enumerate(COARSE_SIDES):
            @pl.when(inside(-dw, 0))
            def _():
                coarse_copy(k, chin, chout, cs, cr, w - dw).wait_recv()

            @pl.when(jnp.logical_not(inside(-dw, 0)))
            def _():
                chin[k] = jnp.zeros((chalo, LANES), f32)

        far = wide_halves(jnp.concatenate([chin[k] for k in range(4)], axis=0))
        for i, buffer in enumerate((ga, gb)):
            part = slice(i * unit, (i + 1) * unit)
            h = jnp.maximum(buffer[...] + fold(dot(cohh[part, :], far)), 0.0)
            fresh = ce[part, :] + normed(mm(h, weight(s, EDGE_OUT)))
            if keep:
                ce[part, :] = fresh
            wide = wide_halves(fresh)
            for t in range(unit // cper_tile):
                q = (i * (unit // cper_tile) + t) * LANES
                cagg[q : q + LANES, :] = fold(
                    dot(cohs[q : q + LANES, :], wide[t * cper_tile : (t + 1) * cper_tile])
                )
        h = jnp.maximum(cxv[...] + mm(cagg[...], weight(s, NODE_SUM)), 0.0)
        fresh = cx[...] + normed(mm(h, weight(s, NODE_OUT)))
        if keep:
            for d in (2, 1, 3):
                gather_copy(d, n, peer(2 * d)).wait_send()
                gather_copy(chips + d, peer(N - 2 * d), pair).wait_send()
            gather_copy(0, n, pair).wait_send()
            cx[...] = fresh
        else:
            cfull[...] = fresh

    coarse_step(1, chin1, chout1, c1s, c1r, True)
    coarse_step(2, chin2, chout2, c2s, c2r, False)

    cstore = pltpu.make_async_copy(cfull, cout, local_sem.at[7])
    cstore.start()
    cwide = wide_halves(cfull[...])
    for b in range(nodes // 1024):
        part = slice(b * 1024, (b + 1) * 1024)
        total = dot(amat[part, 0:cown], cwide) + dot(amat[part, cown:], cwide)
        x[part, :] = x[part, :] + fold(total)

    take_lists(send, x, hout2)
    for k in range(8):
        fine_start(k, hout2, hin2, h2s, h2r)
    fine_own(3)
    fine_base(3, False)
    fine_halo_in(3, hout2, hin2, h2s, h2r)

    def write_nodes(part, value):
        agg[part, :] = value

    fine_edges_nodes(3, False, write_nodes)
    store = pltpu.make_async_copy(agg, out, local_sem.at[0])
    store.start()

    for k in range(8):
        fine_sent(k, hout1, hin1, h1s, h1r)
        fine_sent(k, hout2, hin2, h2s, h2r)
    for d in range(1, N):
        weight_copy(d, peer(d)).wait_send()
    for i in range(chips):
        pair_copy(i, 2 * i + 1 - core).wait_send()
    for d in (2, 1, 3):
        cross_copy(d, 2 * lax.rem(chip + d, chips) + core, peer(2 * d)).wait_send()
    for k, dw in enumerate(COARSE_SIDES):
        @pl.when(inside(dw, 0))
        def _():
            coarse_copy(k, chin1, chout1, c1s, c1r, w + dw).wait_send()
            coarse_copy(k, chin2, chout2, c2s, c2r, w + dw).wait_send()
    cstore.wait()
    store.wait()


def local(
    W, N,
    fine_nodes, fine_edges, fine_sender, fine_offset, fine_send,
    coarse_edges, coarse_sender, coarse_offset, coarse_send,
    restrict_source, restrict_offset, restrict_tile, restrict_weight,
    prolong_index, prolong_weight, restrict_table, prolong_table,
    edge_w1, edge_w2, node_w1, node_w2,
):
    nodes, slots = fine_nodes.shape[0], fine_edges.shape[0]
    halo, chalo = fine_send.shape[2], coarse_send.shape[2]
    tiles = nodes // LANES
    per_tile = slots // tiles
    cown = N * LANES
    cslots = coarse_edges.shape[0]
    blocks = restrict_tile.shape[0]
    smem = pl.BlockSpec(memory_space=pltpu.SMEM)
    vmem = pl.BlockSpec(memory_space=pltpu.VMEM)
    hbm = pl.BlockSpec(memory_space=pl.ANY)

    def F(*shape):
        return pltpu.VMEM(shape, f32)

    def B(*shape):
        return pltpu.VMEM(shape, bf16)

    def D(count):
        return pltpu.SemaphoreType.DMA((count,))

    row = lambda flat: flat.reshape(-1, LANES)
    return pl.pallas_call(
        functools.partial(kernel, (W, N)),
        out_shape=(
            jax.ShapeDtypeStruct((nodes, LANES), f32),
            jax.ShapeDtypeStruct((cown, LANES), f32),
        ),
        in_specs=[smem] * 8 + [vmem] * 7 + [hbm] * 7,
        out_specs=(hbm, hbm),
        scratch_shapes=[
            F(nodes, LANES), F(slots, LANES), F(slots, LANES), F(nodes + 8 * halo, LANES),
            B(nodes, 2 * LANES), F(nodes, LANES), F(nodes, LANES),
            F(4 * per_tile, LANES), F(4 * per_tile, LANES),
            B(slots, LANES), B(nodes, per_tile), B(28, 2 * LANES, 2 * LANES),
            F(*edge_w1.shape), F(*edge_w2.shape), F(*node_w1.shape), F(*node_w2.shape),
            F(8, halo, LANES), F(8, halo, LANES), F(8, halo, LANES), F(8, halo, LANES),
            F(blocks, LANES), B(LANES, blocks * LANES), B(16, blocks * LANES), F(blocks * LANES, LANES),
            F(blocks, LANES, LANES), F(N, LANES, LANES), F(N, LANES, LANES),
            F(N, 8, LANES), F(N, 8, LANES),
            F(cown, LANES), F(cslots, LANES), F(cslots, LANES), F(cown + 4 * chalo, LANES),
            B(cslots, LANES), B(cown, cslots // (cown // LANES)), B(cslots, 4 * chalo),
            F(4, chalo, LANES), F(4, chalo, LANES), F(4, chalo, LANES), F(4, chalo, LANES), F(4, chalo, LANES),
            B(cown, 2 * LANES), F(cown, LANES), F(cown, LANES), F(cown, LANES),
            B(nodes, 2 * cown),
            D(8), D(8), D(8), D(8), D(8), D(N), D(N), D(N), D(N),
            D(N), D(N), D(4), D(4), D(4), D(4),
        ],
        compiler_params=pltpu.CompilerParams(
            collective_id=0, has_side_effects=True, vmem_limit_bytes=60 << 20
        ),
        name="graph_window",
    )(
        fine_sender, fine_send, coarse_sender, coarse_send, restrict_source, restrict_tile,
        restrict_table, prolong_table,
        row(fine_offset), row(coarse_offset), row(coarse_sender), row(restrict_offset), row(restrict_weight),
        prolong_index, prolong_weight,
        fine_nodes, fine_edges, coarse_edges, edge_w1, edge_w2, node_w1, node_w2,
    )


def solution(mesh):
    both = ("wide", "narrow")
    placed = (
        P(both, None), P(both, None), P(both), P(both), P(both, None, None),
        P("wide", None), P("wide"), P("wide"), P("wide", None, None),
        P(both), P(both), P(both), P(both), P(None, both), P(None, both),
        P(), P(), P(), P(), P(), P(),
    )
    return jax.shard_map(
        functools.partial(local, mesh.shape["wide"], mesh.shape["narrow"]),
        mesh=mesh,
        in_specs=placed,
        out_specs=(P(both, None), P("wide", None)),
        check_vma=False,
    )
```

```python
import functools

import jax
import jax.numpy as jnp
from jax import lax
from jax.experimental import pallas as pl
from jax.experimental.pallas import tpu as pltpu
from jax.sharding import PartitionSpec as P

MESH = pl.DeviceIdType.MESH
f32, bf16, i32 = jnp.float32, jnp.bfloat16, jnp.int32
LANES = 128
CHUNK = 256
FINE_SIDES = ((-1, -1), (-1, 0), (-1, 1), (0, -1), (0, 1), (1, -1), (1, 0), (1, 1))
COARSE_SIDES = (-2, -1, 1, 2)
EDGE_OWN, EDGE_FROM, EDGE_TO, EDGE_OUT, NODE_OWN, NODE_SUM, NODE_OUT = range(7)


def halves(values):
    high = values.astype(bf16)
    return high, (values - high.astype(f32)).astype(bf16)


def wide_halves(values):
    return jnp.concatenate(halves(values), axis=1)


def fold(product):
    return product[:, :LANES] + product[:, LANES:]


def dot(left, right):
    return jnp.dot(left, right, preferred_element_type=f32)


def mm(values, weight):
    return fold(dot(wide_halves(values), weight))


def normed(centered):
    return centered * lax.rsqrt(jnp.mean(centered * centered, axis=-1, keepdims=True) + 1e-05)


def as_columns(row):
    return jnp.broadcast_to(row, (LANES, LANES)).T


def lookup(levels, table):
    found = jnp.zeros(levels.shape, f32)
    for level in range(table.shape[0]):
        found = jnp.where(levels == level, table[level], found)
    return found


def sub_iota(shape):
    return lax.broadcasted_iota(i32, shape, 0)


def lane_iota(shape):
    return lax.broadcasted_iota(i32, shape, 1)


def span(start, size):
    return pl.ds(pl.multiple_of(start, size), size)


def take_rows(index, start, count, table, out):
    window = index.shape[0] - CHUNK + 1

    def some(b, carry):
        first = pl.multiple_of(b * CHUNK, CHUNK)
        there = out.at[pl.ds(first, CHUNK)]
        for j in range(CHUNK):
            place = index.at[pl.ds(j, window)][start + first]
            there[pl.ds(j, 1), :] = table[pl.ds(place, 1), :]
        return carry

    lax.fori_loop(0, count // CHUNK, some, 0)


def take_lists(lists, table, out):
    count, length = out.shape[0], out.shape[1]

    def one(k, carry):
        there = out.at[k]
        for j in range(length):
            there[pl.ds(j, 1), :] = table[pl.ds(lists[0, k, j], 1), :]
        return carry

    lax.fori_loop(0, count, one, 0)


def place_of():
    return lax.axis_index("wide"), lax.axis_index("narrow")


def remote_copy(src, dst, send_sem, recv_sem, where):
    return pltpu.make_async_remote_copy(
        src_ref=src, dst_ref=dst, send_sem=send_sem, recv_sem=recv_sem,
        device_id=where, device_id_type=MESH,
    )


def greetings():
    barrier = pltpu.get_barrier_semaphore()

    def signal(where):
        pl.semaphore_signal(barrier, inc=1, device_id=where, device_id_type=MESH)

    return signal, lambda count: pl.semaphore_wait(barrier, count)


def kernel(
    sizes,
    sender, send, csender, csend, rsource, rtile, rtable, ptable,
    foff, coff, crow, roff, rlevel, pindex, plevel,
    x_in, e_in, ce_in, ew1, ew2, nw1, nw2,
    xout, xvout, aggout, wout, cout,
    x, e, base, table, xc, xv, agg, ga, ohg, ohs, wd,
    r_ew1, r_ew2, r_nw1, r_nw2,
    hout1, hin1, hout2, hin2,
    scale, roh, rsel, picked, contrib, rs_out, rs_in, dd_out, dd_in,
    cx, ce, cbase, ctable, cohg, cohs, cohh, cpick, chout1, chout2, chin1, chin2, cxc, cxv, cagg, cfull,
    amat,
    local_sem, h1s, h1r, h2s, h2r, rss, rsr, dds, ddr, ags, agr,
    c1s, c1r, c2s, c2r,
):
    W, N = sizes
    w, n = place_of()
    nodes, slots = x.shape[0], e.shape[0]
    halo = send.shape[2]
    tiles = nodes // LANES
    per_tile = slots // tiles
    unit = 8 * per_tile
    cown = cfull.shape[0]
    chalo = csend.shape[2]
    cslots = ce.shape[0]
    blocks = rsource.shape[0] // LANES

    def inside(dw, dn):
        return (w + dw >= 0) & (w + dw < W) & (n + dn >= 0) & (n + dn < N)

    def remote(src, dst, send_sem, recv_sem, where):
        return remote_copy(src, dst, send_sem, recv_sem, where)

    def peer(d):
        return lax.rem(n + d, N)

    loads = [
        pltpu.make_async_copy(x_in, x, local_sem.at[0]),
        pltpu.make_async_copy(ew1, r_ew1, local_sem.at[1]),
        pltpu.make_async_copy(ew2, r_ew2, local_sem.at[2]),
        pltpu.make_async_copy(nw1, r_nw1, local_sem.at[3]),
        pltpu.make_async_copy(nw2, r_nw2, local_sem.at[4]),
        pltpu.make_async_copy(e_in, e, local_sem.at[5]),
        pltpu.make_async_copy(ce_in, ce, local_sem.at[6]),
    ]
    loads[0].start()

    signal, wait_for = greetings()
    others = [(dw, dn) for dw, dn in FINE_SIDES if dw] + [(-2, 0), (2, 0)]
    for d in range(1, N):
        signal((w, peer(d)))
    expected = i32(N - 1)
    for dw, dn in others:
        @pl.when(inside(dw, dn))
        def _():
            signal((w + dw, n + dn))
        expected = expected + inside(dw, dn).astype(i32)

    def fine_copy(k, hout, hin, ss, rs, where):
        return remote(hout.at[k], hin.at[k], ss.at[k], rs.at[k], where)

    def send_halo(hout, hin, ss, rs):
        def one(k, carry):
            there = hout.at[k]
            for j in range(halo):
                there[pl.ds(j, 1), :] = x[pl.ds(send[0, k, j], 1), :]
            square = jnp.where(k >= 4, k + 1, k)
            dw, dn = lax.div(square, 3) - 1, lax.rem(square, 3) - 1

            @pl.when(inside(dw, dn))
            def _():
                fine_copy(k, hout, hin, ss, rs, (w + dw, n + dn)).start()

            return carry

        lax.fori_loop(0, 8, one, 0)

    def fine_arrive(k, hout, hin, ss, rs):
        dw, dn = FINE_SIDES[k]

        @pl.when(inside(-dw, -dn))
        def _():
            fine_copy(k, hout, hin, ss, rs, (w - dw, n - dn)).wait_recv()

        @pl.when(jnp.logical_not(inside(-dw, -dn)))
        def _():
            hin[k] = jnp.zeros(hin.shape[1:], f32)

    def fine_sent(k, hout, hin, ss, rs):
        dw, dn = FINE_SIDES[k]

        @pl.when(inside(dw, dn))
        def _():
            fine_copy(k, hout, hin, ss, rs, (w + dw, n + dn)).wait_send()

    loads[0].wait()
    for load in loads[1:]:
        load.start()
    wait_for(expected)
    send_halo(hout1, hin1, h1s, h1r)

    for load in loads[1:5]:
        load.wait()

    def put_weight(section, place, value):
        high, low = halves(value)
        wide = jnp.concatenate([high, low], axis=1)
        wd[section * 7 + place] = jnp.concatenate([wide, wide], axis=0)

    def center(value):
        return value - jnp.mean(value, axis=1, keepdims=True)

    def prepare(s):
        put_weight(s, EDGE_OWN, r_ew1[s, 0:128, :])
        put_weight(s, EDGE_FROM, r_ew1[s, 128:256, :])
        put_weight(s, EDGE_TO, r_ew1[s, 256:384, :])
        put_weight(s, EDGE_OUT, center(r_ew2[s]))
        put_weight(s, NODE_OWN, r_nw1[s, 0:128, :])
        put_weight(s, NODE_SUM, r_nw1[s, 128:256, :])
        put_weight(s, NODE_OUT, center(r_nw2[s]))

    prepare(0)

    def weight(s, place):
        return wd[s * 7 + place]

    lanes = lane_iota((LANES, LANES))
    rows = sub_iota((LANES, LANES))
    per_block = per_tile // LANES

    def one_hots(t, carry):
        for c in range(per_block):
            row = foff[pl.ds(t * per_block + c, 1), :]
            to = as_columns(jnp.minimum(row, LANES - 1))
            ohg[span(t * per_tile + c * LANES, LANES), :] = (to == lanes).astype(f32).astype(bf16)
            ohs[span(t * LANES, LANES), c * LANES : (c + 1) * LANES] = (
                (rows == row).astype(f32).astype(bf16)
            )
        return carry

    lax.fori_loop(0, tiles, one_hots, 0, unroll=4)

    def fine_own(s):
        for b in range(nodes // 1024):
            part = slice(b * 1024, (b + 1) * 1024)
            wide = wide_halves(x[part, :])
            table[part, :] = fold(dot(wide, weight(s, EDGE_FROM)))
            xc[part, :] = wide_halves(fold(dot(wide, weight(s, EDGE_TO))))
            xv[part, :] = fold(dot(wide, weight(s, NODE_OWN)))

    def fine_base_edges(s):
        def one(i, carry):
            part = span(i * unit, unit)
            base[part, :] = mm(e[part, :], weight(s, EDGE_OWN))
            return carry

        lax.fori_loop(0, slots // unit, one, 0)

    def fine_base(s, with_edges):
        def one(i, carry):
            part = span(i * unit, unit)
            own = mm(e[part, :], weight(s, EDGE_OWN)) if with_edges else base[part, :]
            to = []
            for t in range(unit // per_tile):
                here = ohg[span(i * unit + t * per_tile, per_tile), :]
                there = xc[span((i * (unit // per_tile) + t) * LANES, LANES), :]
                to.append(fold(dot(here, there)))
            base[part, :] = own + jnp.concatenate(to, axis=0)
            return carry

        lax.fori_loop(0, slots // unit, one, 0)

    def fine_halo_in(s, hout, hin, ss, rs):
        for k in range(8):
            fine_arrive(k, hout, hin, ss, rs)
        rows_in = jnp.concatenate([hin[k] for k in range(8)], axis=0)
        table[nodes:, :] = mm(rows_in, weight(s, EDGE_FROM))

    def fine_edges_sums(s, keep):
        take_rows(sender, 0, slots, table, ga)
        h = jnp.maximum(base[...] + ga[...], 0.0)
        fresh = e[...] + normed(mm(h, weight(s, EDGE_OUT)))
        if keep:
            e[...] = fresh
        wide = wide_halves(fresh)
        for t in range(tiles):
            q = slice(t * LANES, (t + 1) * LANES)
            agg[q, :] = fold(dot(ohs[q, :], wide[t * per_tile : (t + 1) * per_tile]))

    def fine_nodes_update(s):
        for b in range(nodes // 1024):
            part = slice(b * 1024, (b + 1) * 1024)
            h = jnp.maximum(xv[part, :] + mm(agg[part, :], weight(s, NODE_SUM)), 0.0)
            x[part, :] = x[part, :] + normed(mm(h, weight(s, NODE_OUT)))

    fine_own(0)
    loads[5].wait()
    fine_base(0, True)
    fine_halo_in(0, hout1, hin1, h1s, h1r)

    fine_edges_sums(0, True)
    fine_nodes_update(0)

    scale[...] = lookup(rlevel[...], rtable)

    take_rows(rsource, 0, blocks * LANES, x, picked)

    def restrict_block(b, carry):
        row = roff[pl.ds(b, 1), :]
        hit = rows == row
        roh[:, span(b * LANES, LANES)] = hit.astype(f32).astype(bf16)
        left = wide_halves(jnp.where(hit, scale[pl.ds(b, 1), :], 0.0))
        right = wide_halves(picked[span(b * LANES, LANES), :])
        contrib[b] = fold(dot(left, jnp.concatenate([right, right], axis=0)))
        return carry

    lax.fori_loop(0, blocks, restrict_block, 0, unroll=20)

    def restrict_tile(t):
        def add(b, total):
            return total + contrib[b] * (rtile[b] == t).astype(f32)

        rs_out[t] = lax.fori_loop(0, blocks, add, jnp.zeros((LANES, LANES), f32), unroll=8)

    core, chip = lax.rem(n, 2), lax.div(n, 2)
    pair = n + 1 - 2 * core
    chips = N // 2

    def pair_copy(i, tile):
        return remote(rs_out.at[tile], rs_in.at[i], rss.at[i], rsr.at[i], (w, pair))

    def cross_copy(d, tile, toward):
        slot = chips + d
        return remote(rs_out.at[tile], rs_in.at[slot], rss.at[slot], rsr.at[slot], (w, toward))

    for i in range(chips):
        restrict_tile(2 * i + 1 - core)
        pair_copy(i, 2 * i + 1 - core).start()

    def select_block(b, carry):
        kept = jnp.where(sub_iota((8, LANES)) == rtile[b], scale[pl.ds(b, 1), :], 0.0)
        high = kept.astype(bf16).astype(f32)
        rsel[:, span(b * LANES, LANES)] = jnp.concatenate([high, kept - high], axis=0).astype(bf16)
        return carry

    lax.fori_loop(0, blocks, select_block, 0, unroll=8)
    weights = lax.dot_general(
        rsel[...], roh[...], (((1,), (1,)), ((), ())), preferred_element_type=f32
    )
    weights = weights[0:8] + weights[8:16]
    for t in range(N):
        dd_out[t] = jnp.broadcast_to(weights[t : t + 1], (8, LANES))

    def weight_copy(d, toward):
        return remote(dd_out.at[peer(d)], dd_in.at[d], dds.at[d], ddr.at[d], (w, toward))

    for d in range(1, N):
        weight_copy(d, peer(d)).start()
    for i in range(chips):
        restrict_tile(2 * i + core)
    for d in (2, 1, 3, 0):
        place = lax.rem(chip + d, chips)
        tile = 2 * place + core
        pair_copy(place, tile).wait_recv()
        rs_out[tile] = rs_out[tile] + rs_in[place]
        if d:
            cross_copy(d, tile, peer(2 * d)).start()

    cper_tile = cslots // (cown // LANES)

    def coarse_base_edges(s):
        cbase[...] = mm(ce[...], weight(s, EDGE_OWN))

    prepare(1)

    def prolong_block(b, carry):
        part = span(b * LANES, LANES)
        raw = [lookup(plevel[k : k + 1, part], ptable) for k in range(3)]
        total = raw[0] + raw[1] + raw[2]
        places = [as_columns(pindex[k : k + 1, part]) for k in range(3)]
        amounts = [as_columns(r / total) for r in raw]
        for c in range(cown // LANES):
            value = jnp.zeros((LANES, LANES), f32)
            for k in range(3):
                value = value + jnp.where(places[k] == lanes + c * LANES, amounts[k], 0.0)
            high, low = halves(value)
            amat[part, c * LANES : (c + 1) * LANES] = high
            amat[part, cown + c * LANES : cown + (c + 1) * LANES] = low
        return carry

    def prolong_weights(part):
        lax.fori_loop(part * tiles // 4, (part + 1) * tiles // 4, prolong_block, 0, unroll=2)

    def coarse_one_hots(t, carry):
        for c in range(cper_tile // LANES):
            block = t * (cper_tile // LANES) + c
            row = coff[pl.ds(block, 1), :]
            part = span(block * LANES, LANES)
            cohg[part, :] = (as_columns(jnp.minimum(row, LANES - 1)) == lanes).astype(f32).astype(bf16)
            cohs[span(t * LANES, LANES), c * LANES : (c + 1) * LANES] = (
                (rows == row).astype(f32).astype(bf16)
            )
            origin = as_columns(crow[pl.ds(block, 1), :]) - cown
            for h in range(4 * chalo // LANES):
                cohh[part, h * LANES : (h + 1) * LANES] = (
                    (origin == lanes + h * LANES).astype(f32).astype(bf16)
                )
        return carry

    lax.fori_loop(0, cown // LANES, coarse_one_hots, 0, unroll=2)
    ctable[cown:, :] = jnp.zeros((4 * chalo, LANES), f32)
    loads[6].wait()
    prolong_weights(0)
    prolong_weights(1)

    own = span(n * LANES, LANES)
    numer = rs_out[n]
    for d in range(1, chips):
        cross_copy(d, n, peer(N - 2 * d)).wait_recv()
        numer = numer + rs_in[chips + d]
    denom = dd_out[n]
    for d in range(1, N):
        weight_copy(d, peer(N - d)).wait_recv()
        denom = denom + dd_in[d]
    cx[own, :] = numer / (1.0 + as_columns(denom[0:1]))

    def gather_copy(slot, tile, toward):
        place = cx.at[span(tile * LANES, LANES)]
        return remote(place, place, ags.at[slot], agr.at[slot], (w, toward))

    for d in (2, 1, 3):
        gather_copy(d, n, peer(2 * d)).start()
    gather_copy(0, n, pair).start()
    prepare(2)
    prepare(3)
    prolong_weights(2)
    fine_base_edges(3)
    coarse_base_edges(1)
    for d in (1, 3, 2):
        tile = peer(N - 2 * d)
        gather_copy(d, tile, tile).wait_recv()
        gather_copy(chips + d, tile, pair).start()
    prolong_weights(3)
    gather_copy(0, pair, pair).wait_recv()
    for d in (1, 3, 2):
        gather_copy(chips + d, lax.rem(pair + N - 2 * d, N), pair).wait_recv()

    cg = ga.at[pl.ds(0, cslots)]

    def coarse_copy(k, chin, chout, ss, rs, toward):
        return remote(chout.at[k], chin.at[k], ss.at[k], rs.at[k], (toward, n))

    def coarse_step(s, chin, chout, cs, cr, keep):
        take_lists(csend, cx, cpick)
        for k in range(4):
            chout[k] = mm(cpick[k], weight(s, EDGE_FROM))
        for k, dw in enumerate(COARSE_SIDES):
            @pl.when(inside(dw, 0))
            def _():
                coarse_copy(k, chin, chout, cs, cr, w + dw).start()

        wide = wide_halves(cx[...])
        ctable[0:cown, :] = fold(dot(wide, weight(s, EDGE_FROM)))
        cxc[...] = wide_halves(fold(dot(wide, weight(s, EDGE_TO))))
        cxv[...] = fold(dot(wide, weight(s, NODE_OWN)))
        if s != 1:
            coarse_base_edges(s)
        take_rows(csender, 0, cslots, ctable, cg)
        to = []
        for t in range(cown // LANES):
            here = cohg[t * cper_tile : (t + 1) * cper_tile, :]
            to.append(fold(dot(here, cxc[t * LANES : (t + 1) * LANES, :])))
        cg[...] = cg[...] + (cbase[...] + jnp.concatenate(to, axis=0))
        for k, dw in enumerate(COARSE_SIDES):
            @pl.when(inside(-dw, 0))
            def _():
                coarse_copy(k, chin, chout, cs, cr, w - dw).wait_recv()

            @pl.when(jnp.logical_not(inside(-dw, 0)))
            def _():
                chin[k] = jnp.zeros((chalo, LANES), f32)

        far = wide_halves(jnp.concatenate([chin[k] for k in range(4)], axis=0))
        h = jnp.maximum(cg[...] + fold(dot(cohh[...], far)), 0.0)
        fresh = ce[...] + normed(mm(h, weight(s, EDGE_OUT)))
        if keep:
            ce[...] = fresh
        wide = wide_halves(fresh)
        for t in range(cown // LANES):
            q = slice(t * LANES, (t + 1) * LANES)
            cagg[q, :] = fold(dot(cohs[q, :], wide[t * cper_tile : (t + 1) * cper_tile]))
        h = jnp.maximum(cxv[...] + mm(cagg[...], weight(s, NODE_SUM)), 0.0)
        fresh = cx[...] + normed(mm(h, weight(s, NODE_OUT)))
        if keep:
            for d in (2, 1, 3):
                gather_copy(d, n, peer(2 * d)).wait_send()
                gather_copy(chips + d, peer(N - 2 * d), pair).wait_send()
            gather_copy(0, n, pair).wait_send()
            cx[...] = fresh
        else:
            cfull[...] = fresh

    coarse_step(1, chin1, chout1, c1s, c1r, True)
    coarse_step(2, chin2, chout2, c2s, c2r, False)

    cstore = pltpu.make_async_copy(cfull, cout, local_sem.at[7])
    cstore.start()
    cwide = wide_halves(cfull[...])
    for b in range(nodes // 1024):
        part = slice(b * 1024, (b + 1) * 1024)
        total = dot(amat[part, 0:cown], cwide) + dot(amat[part, cown:], cwide)
        x[part, :] = x[part, :] + fold(total)

    send_halo(hout2, hin2, h2s, h2r)
    xstore = pltpu.make_async_copy(x, xout, local_sem.at[0])
    xstore.start()
    fine_own(3)
    xvstore = pltpu.make_async_copy(xv, xvout, local_sem.at[1])
    xvstore.start()
    wstore = pltpu.make_async_copy(wd.at[pl.ds(3 * 7 + NODE_SUM, 2)], wout, local_sem.at[2])
    wstore.start()
    fine_base(3, False)
    fine_halo_in(3, hout2, hin2, h2s, h2r)

    fine_edges_sums(3, False)
    store = pltpu.make_async_copy(agg, aggout, local_sem.at[3])
    store.start()

    for k in range(8):
        fine_sent(k, hout1, hin1, h1s, h1r)
        fine_sent(k, hout2, hin2, h2s, h2r)
    for d in range(1, N):
        weight_copy(d, peer(d)).wait_send()
    for i in range(chips):
        pair_copy(i, 2 * i + 1 - core).wait_send()
    for d in (2, 1, 3):
        cross_copy(d, 2 * lax.rem(chip + d, chips) + core, peer(2 * d)).wait_send()
    for k, dw in enumerate(COARSE_SIDES):
        @pl.when(inside(dw, 0))
        def _():
            coarse_copy(k, chin1, chout1, c1s, c1r, w + dw).wait_send()
            coarse_copy(k, chin2, chout2, c2s, c2r, w + dw).wait_send()
    cstore.wait()
    xstore.wait()
    xvstore.wait()
    wstore.wait()
    store.wait()


def last_nodes(x, xv, agg, weights, coarse, out, coarse_out):
    h = jnp.maximum(xv[...] + mm(agg[...], weights[0]), 0.0)
    out[...] = x[...] + normed(mm(h, weights[1]))
    coarse_out[...] = coarse[...]


def local(
    W, N,
    fine_nodes, fine_edges, fine_sender, fine_offset, fine_send,
    coarse_edges, coarse_sender, coarse_offset, coarse_send,
    restrict_source, restrict_offset, restrict_tile, restrict_weight,
    prolong_index, prolong_weight, restrict_table, prolong_table,
    edge_w1, edge_w2, node_w1, node_w2,
):
    nodes, slots = fine_nodes.shape[0], fine_edges.shape[0]
    halo, chalo = fine_send.shape[2], coarse_send.shape[2]
    tiles = nodes // LANES
    per_tile = slots // tiles
    cown = N * LANES
    cslots = coarse_edges.shape[0]
    blocks = restrict_tile.shape[0]
    smem = pl.BlockSpec(memory_space=pltpu.SMEM)
    vmem = pl.BlockSpec(memory_space=pltpu.VMEM)
    hbm = pl.BlockSpec(memory_space=pl.ANY)

    def F(*shape):
        return pltpu.VMEM(shape, f32)

    def B(*shape):
        return pltpu.VMEM(shape, bf16)

    def D(count):
        return pltpu.SemaphoreType.DMA((count,))

    row = lambda flat: flat.reshape(-1, LANES)
    parts = pl.pallas_call(
        functools.partial(kernel, (W, N)),
        out_shape=(
            jax.ShapeDtypeStruct((nodes, LANES), f32),
            jax.ShapeDtypeStruct((nodes, LANES), f32),
            jax.ShapeDtypeStruct((nodes, LANES), f32),
            jax.ShapeDtypeStruct((2, 2 * LANES, 2 * LANES), bf16),
            jax.ShapeDtypeStruct((cown, LANES), f32),
        ),
        in_specs=[smem] * 8 + [vmem] * 7 + [hbm] * 7,
        out_specs=(hbm,) * 5,
        scratch_shapes=[
            F(nodes, LANES), F(slots, LANES), F(slots, LANES), F(nodes + 8 * halo, LANES),
            B(nodes, 2 * LANES), F(nodes, LANES), F(nodes, LANES),
            F(slots, LANES),
            B(slots, LANES), B(nodes, per_tile), B(28, 2 * LANES, 2 * LANES),
            F(*edge_w1.shape), F(*edge_w2.shape), F(*node_w1.shape), F(*node_w2.shape),
            F(8, halo, LANES), F(8, halo, LANES), F(8, halo, LANES), F(8, halo, LANES),
            F(blocks, LANES), B(LANES, blocks * LANES), B(16, blocks * LANES), F(blocks * LANES, LANES),
            F(blocks, LANES, LANES), F(N, LANES, LANES), F(N, LANES, LANES),
            F(N, 8, LANES), F(N, 8, LANES),
            F(cown, LANES), F(cslots, LANES), F(cslots, LANES), F(cown + 4 * chalo, LANES),
            B(cslots, LANES), B(cown, cslots // (cown // LANES)), B(cslots, 4 * chalo),
            F(4, chalo, LANES), F(4, chalo, LANES), F(4, chalo, LANES), F(4, chalo, LANES), F(4, chalo, LANES),
            B(cown, 2 * LANES), F(cown, LANES), F(cown, LANES), F(cown, LANES),
            B(nodes, 2 * cown),
            D(8), D(8), D(8), D(8), D(8), D(N), D(N), D(N), D(N),
            D(N), D(N), D(4), D(4), D(4), D(4),
        ],
        compiler_params=pltpu.CompilerParams(
            collective_id=0, has_side_effects=True, vmem_limit_bytes=60 << 20
        ),
        name="graph_window",
    )(
        fine_sender, fine_send, coarse_sender, coarse_send, restrict_source, restrict_tile,
        restrict_table, prolong_table,
        row(fine_offset), row(coarse_offset), row(coarse_sender), row(restrict_offset), row(restrict_weight),
        prolong_index, prolong_weight,
        fine_nodes, fine_edges, coarse_edges, edge_w1, edge_w2, node_w1, node_w2,
    )
    steps = 2
    fine_rows = pl.BlockSpec((nodes // steps, LANES), lambda i: (i, 0))
    coarse_rows = pl.BlockSpec((cown // steps, LANES), lambda i: (i, 0))
    return pl.pallas_call(
        last_nodes,
        grid=(steps,),
        out_shape=(
            jax.ShapeDtypeStruct((nodes, LANES), f32),
            jax.ShapeDtypeStruct((cown, LANES), f32),
        ),
        in_specs=[fine_rows] * 3 + [vmem, coarse_rows],
        out_specs=(fine_rows, coarse_rows),
        compiler_params=pltpu.CompilerParams(vmem_limit_bytes=60 << 20),
        name="last_nodes",
    )(*parts)


def solution(mesh):
    both = ("wide", "narrow")
    placed = (
        P(both, None), P(both, None), P(both), P(both), P(both, None, None),
        P("wide", None), P("wide"), P("wide"), P("wide", None, None),
        P(both), P(both), P(both), P(both), P(None, both), P(None, both),
        P(), P(), P(), P(), P(), P(),
    )
    return jax.shard_map(
        functools.partial(local, mesh.shape["wide"], mesh.shape["narrow"]),
        mesh=mesh,
        in_specs=placed,
        out_specs=(P(both, None), P("wide", None)),
        check_vma=False,
    )
```

```python
import functools

import jax
import jax.numpy as jnp
from jax import lax
from jax.experimental import pallas as pl
from jax.experimental.pallas import tpu as pltpu
from jax.sharding import PartitionSpec as P

MESH = pl.DeviceIdType.MESH
f32, bf16, i32 = jnp.float32, jnp.bfloat16, jnp.int32
LANES = 128
CHUNK = 256
FINE_SIDES = ((-1, -1), (-1, 0), (-1, 1), (0, -1), (0, 1), (1, -1), (1, 0), (1, 1))
COARSE_SIDES = (-2, -1, 1, 2)
EDGE_OWN, EDGE_FROM, EDGE_TO, EDGE_OUT, NODE_OWN, NODE_SUM, NODE_OUT = range(7)


def halves(values):
    high = values.astype(bf16)
    return high, (values - high.astype(f32)).astype(bf16)


def wide_halves(values):
    return jnp.concatenate(halves(values), axis=1)


def fold(product):
    return product[:, :LANES] + product[:, LANES:]


def dot(left, right):
    return jnp.dot(left, right, preferred_element_type=f32)


def mm(values, weight):
    return fold(dot(wide_halves(values), weight))


def normed(centered):
    spread = jnp.sum(centered * centered, axis=-1, keepdims=True) * (1.0 / LANES)
    return centered * lax.rsqrt(spread + 1e-05)


def as_columns(row):
    return jnp.broadcast_to(row, (LANES, LANES)).T


def lookup(levels, table):
    found = jnp.zeros(levels.shape, f32)
    for level in range(table.shape[0]):
        found = jnp.where(levels == level, table[level], found)
    return found


def sub_iota(shape):
    return lax.broadcasted_iota(i32, shape, 0)


def lane_iota(shape):
    return lax.broadcasted_iota(i32, shape, 1)


def span(start, size):
    return pl.ds(pl.multiple_of(start, size), size)


def take_rows(index, start, count, table, out):
    window = index.shape[0] - CHUNK + 1

    def some(b, carry):
        first = pl.multiple_of(b * CHUNK, CHUNK)
        there = out.at[pl.ds(first, CHUNK)]
        for j in range(CHUNK):
            place = index.at[pl.ds(j, window)][start + first]
            there[pl.ds(j, 1), :] = table[pl.ds(place, 1), :]
        return carry

    lax.fori_loop(0, count // CHUNK, some, 0)


def take_lists(lists, table, out):
    count, length = out.shape[0], out.shape[1]

    def one(k, carry):
        there = out.at[k]
        for j in range(length):
            there[pl.ds(j, 1), :] = table[pl.ds(lists[0, k, j], 1), :]
        return carry

    lax.fori_loop(0, count, one, 0)


def place_of():
    return lax.axis_index("wide"), lax.axis_index("narrow")


def remote_copy(src, dst, send_sem, recv_sem, where):
    return pltpu.make_async_remote_copy(
        src_ref=src, dst_ref=dst, send_sem=send_sem, recv_sem=recv_sem,
        device_id=where, device_id_type=MESH,
    )


def greetings():
    barrier = pltpu.get_barrier_semaphore()

    def signal(where):
        pl.semaphore_signal(barrier, inc=1, device_id=where, device_id_type=MESH)

    return signal, lambda count: pl.semaphore_wait(barrier, count)


def kernel(
    sizes,
    sender, send, csender, csend, rsource, rtile, rtable, ptable,
    foff, coff, crow, roff, rlevel, pindex, plevel,
    x_in, e_in, ce_in, ew1, ew2, nw1, nw2,
    xout, xvout, aggout, wout, cout,
    x, e, base, table, xc, xv, agg, ga, ohg, ohs, wd,
    r_ew1, r_ew2, r_nw1, r_nw2,
    hout1, hin1, hout2, hin2,
    scale, roh, rsel, picked, contrib, rs_out, rs_in, dd_out, dd_in,
    cx, ce, cbase, ctable, cohg, cohs, cohh, cpick, chout1, chout2, chin1, chin2, cxc, cxv, cagg, cfull,
    amat,
    local_sem, h1s, h1r, h2s, h2r, rss, rsr, dds, ddr, ags, agr,
    c1s, c1r, c2s, c2r,
):
    W, N = sizes
    w, n = place_of()
    nodes, slots = x.shape[0], e.shape[0]
    halo = send.shape[2]
    tiles = nodes // LANES
    per_tile = slots // tiles
    unit = 8 * per_tile
    cown = cfull.shape[0]
    chalo = csend.shape[2]
    cslots = ce.shape[0]
    blocks = rsource.shape[0] // LANES

    def inside(dw, dn):
        return (w + dw >= 0) & (w + dw < W) & (n + dn >= 0) & (n + dn < N)

    def remote(src, dst, send_sem, recv_sem, where):
        return remote_copy(src, dst, send_sem, recv_sem, where)

    def peer(d):
        return lax.rem(n + d, N)

    loads = [
        pltpu.make_async_copy(x_in, x, local_sem.at[0]),
        pltpu.make_async_copy(ew1, r_ew1, local_sem.at[1]),
        pltpu.make_async_copy(ew2, r_ew2, local_sem.at[2]),
        pltpu.make_async_copy(nw1, r_nw1, local_sem.at[3]),
        pltpu.make_async_copy(nw2, r_nw2, local_sem.at[4]),
        pltpu.make_async_copy(e_in, e, local_sem.at[5]),
        pltpu.make_async_copy(ce_in, ce, local_sem.at[6]),
    ]
    loads[0].start()

    signal, wait_for = greetings()
    others = [(dw, dn) for dw, dn in FINE_SIDES if dw] + [(-2, 0), (2, 0)]
    for d in range(1, N):
        signal((w, peer(d)))
    expected = i32(N - 1)
    for dw, dn in others:
        @pl.when(inside(dw, dn))
        def _():
            signal((w + dw, n + dn))
        expected = expected + inside(dw, dn).astype(i32)

    def fine_copy(k, hout, hin, ss, rs, where):
        return remote(hout.at[k], hin.at[k], ss.at[k], rs.at[k], where)

    def send_halo(hout, hin, ss, rs, pick):
        def one(k, carry):
            there = hout.at[k]
            for j in range(halo if pick else 0):
                there[pl.ds(j, 1), :] = x[pl.ds(send[0, k, j], 1), :]
            square = jnp.where(k >= 4, k + 1, k)
            dw, dn = lax.div(square, 3) - 1, lax.rem(square, 3) - 1

            @pl.when(inside(dw, dn))
            def _():
                fine_copy(k, hout, hin, ss, rs, (w + dw, n + dn)).start()

            return carry

        lax.fori_loop(0, 8, one, 0)

    def fine_arrive(k, hout, hin, ss, rs):
        dw, dn = FINE_SIDES[k]

        @pl.when(inside(-dw, -dn))
        def _():
            fine_copy(k, hout, hin, ss, rs, (w - dw, n - dn)).wait_recv()

        @pl.when(jnp.logical_not(inside(-dw, -dn)))
        def _():
            hin[k] = jnp.zeros(hin.shape[1:], f32)

    def fine_sent(k, hout, hin, ss, rs):
        dw, dn = FINE_SIDES[k]

        @pl.when(inside(dw, dn))
        def _():
            fine_copy(k, hout, hin, ss, rs, (w + dw, n + dn)).wait_send()

    loads[0].wait()
    for load in loads[1:]:
        load.start()
    take_lists(send, x, hout1)
    wait_for(expected)
    send_halo(hout1, hin1, h1s, h1r, False)

    for load in loads[1:5]:
        load.wait()

    def put_weight(section, place, value):
        high, low = halves(value)
        wide = jnp.concatenate([high, low], axis=1)
        wd[section * 7 + place] = jnp.concatenate([wide, wide], axis=0)

    def center(value):
        return value - jnp.mean(value, axis=1, keepdims=True)

    def prepare(s):
        put_weight(s, EDGE_OWN, r_ew1[s, 0:128, :])
        put_weight(s, EDGE_FROM, r_ew1[s, 128:256, :])
        put_weight(s, EDGE_TO, r_ew1[s, 256:384, :])
        put_weight(s, EDGE_OUT, center(r_ew2[s]))
        put_weight(s, NODE_OWN, r_nw1[s, 0:128, :])
        put_weight(s, NODE_SUM, r_nw1[s, 128:256, :])
        put_weight(s, NODE_OUT, center(r_nw2[s]))

    prepare(0)

    def weight(s, place):
        return wd[s * 7 + place]

    lanes = lane_iota((LANES, LANES))
    rows = sub_iota((LANES, LANES))
    per_block = per_tile // LANES

    def one_hots(t, carry):
        for c in range(per_block):
            row = foff[pl.ds(t * per_block + c, 1), :]
            to = as_columns(jnp.minimum(row, LANES - 1))
            ohg[span(t * per_tile + c * LANES, LANES), :] = (to == lanes).astype(f32).astype(bf16)
            ohs[span(t * LANES, LANES), c * LANES : (c + 1) * LANES] = (
                (rows == row).astype(f32).astype(bf16)
            )
        return carry

    lax.fori_loop(0, tiles, one_hots, 0, unroll=4)

    def fine_own(s):
        for b in range(nodes // 1024):
            part = slice(b * 1024, (b + 1) * 1024)
            wide = wide_halves(x[part, :])
            table[part, :] = fold(dot(wide, weight(s, EDGE_FROM)))
            xc[part, :] = wide_halves(fold(dot(wide, weight(s, EDGE_TO))))
            xv[part, :] = fold(dot(wide, weight(s, NODE_OWN)))

    def fine_base(s):
        def one(i, carry):
            part = span(i * unit, unit)
            own = mm(e[part, :], weight(s, EDGE_OWN))
            to = []
            for t in range(unit // per_tile):
                here = ohg[span(i * unit + t * per_tile, per_tile), :]
                there = xc[span((i * (unit // per_tile) + t) * LANES, LANES), :]
                to.append(fold(dot(here, there)))
            base[part, :] = own + jnp.concatenate(to, axis=0)
            return carry

        lax.fori_loop(0, slots // unit, one, 0)

    def fine_halo_in(s, hout, hin, ss, rs):
        for k in range(8):
            fine_arrive(k, hout, hin, ss, rs)
        rows_in = jnp.concatenate([hin[k] for k in range(8)], axis=0)
        table[nodes:, :] = mm(rows_in, weight(s, EDGE_FROM))

    def fine_edges_sums(s, keep):
        take_rows(sender, 0, slots, table, ga)
        h = jnp.maximum(base[...] + ga[...], 0.0)
        fresh = e[...] + normed(mm(h, weight(s, EDGE_OUT)))
        if keep:
            e[...] = fresh
        wide = wide_halves(fresh)
        for t in range(tiles):
            q = slice(t * LANES, (t + 1) * LANES)
            agg[q, :] = fold(dot(ohs[q, :], wide[t * per_tile : (t + 1) * per_tile]))

    def fine_nodes_update(s):
        for b in range(nodes // 1024):
            part = slice(b * 1024, (b + 1) * 1024)
            h = jnp.maximum(xv[part, :] + mm(agg[part, :], weight(s, NODE_SUM)), 0.0)
            x[part, :] = x[part, :] + normed(mm(h, weight(s, NODE_OUT)))

    fine_own(0)
    loads[5].wait()
    fine_base(0)
    fine_halo_in(0, hout1, hin1, h1s, h1r)

    fine_edges_sums(0, True)
    fine_nodes_update(0)

    scale[...] = lookup(rlevel[...], rtable)

    take_rows(rsource, 0, blocks * LANES, x, picked)

    def restrict_block(b, carry):
        row = roff[pl.ds(b, 1), :]
        hit = rows == row
        roh[:, span(b * LANES, LANES)] = hit.astype(f32).astype(bf16)
        left = wide_halves(jnp.where(hit, scale[pl.ds(b, 1), :], 0.0))
        right = wide_halves(picked[span(b * LANES, LANES), :])
        contrib[b] = fold(dot(left, jnp.concatenate([right, right], axis=0)))
        return carry

    lax.fori_loop(0, blocks, restrict_block, 0, unroll=20)

    def restrict_tile(t):
        def add(b, total):
            return total + contrib[b] * (rtile[b] == t).astype(f32)

        rs_out[t] = lax.fori_loop(0, blocks, add, jnp.zeros((LANES, LANES), f32), unroll=8)

    core, chip = lax.rem(n, 2), lax.div(n, 2)
    pair = n + 1 - 2 * core
    chips = N // 2

    def pair_copy(i, tile):
        return remote(rs_out.at[tile], rs_in.at[i], rss.at[i], rsr.at[i], (w, pair))

    def cross_copy(d, tile, toward):
        slot = chips + d
        return remote(rs_out.at[tile], rs_in.at[slot], rss.at[slot], rsr.at[slot], (w, toward))

    for i in range(chips):
        restrict_tile(2 * i + 1 - core)
        pair_copy(i, 2 * i + 1 - core).start()

    for i in range(chips):
        restrict_tile(2 * i + core)
    for d in (2, 1, 3, 0):
        place = lax.rem(chip + d, chips)
        tile = 2 * place + core
        pair_copy(place, tile).wait_recv()
        rs_out[tile] = rs_out[tile] + rs_in[place]
        if d:
            cross_copy(d, tile, peer(2 * d)).start()

    def select_block(b, carry):
        kept = jnp.where(sub_iota((8, LANES)) == rtile[b], scale[pl.ds(b, 1), :], 0.0)
        high = kept.astype(bf16).astype(f32)
        rsel[:, span(b * LANES, LANES)] = jnp.concatenate([high, kept - high], axis=0).astype(bf16)
        return carry

    lax.fori_loop(0, blocks, select_block, 0, unroll=8)
    weights = lax.dot_general(
        rsel[...], roh[...], (((1,), (1,)), ((), ())), preferred_element_type=f32
    )
    weights = weights[0:8] + weights[8:16]
    for t in range(N):
        dd_out[t] = jnp.broadcast_to(weights[t : t + 1], (8, LANES))

    def weight_copy(d, toward):
        return remote(dd_out.at[peer(d)], dd_in.at[d], dds.at[d], ddr.at[d], (w, toward))

    for d in range(1, N):
        weight_copy(d, peer(d)).start()

    cper_tile = cslots // (cown // LANES)

    def coarse_base_edges(s):
        cbase[...] = mm(ce[...], weight(s, EDGE_OWN))

    prepare(1)

    def prolong_block(b, carry):
        part = span(b * LANES, LANES)
        raw = [lookup(plevel[k : k + 1, part], ptable) for k in range(3)]
        total = raw[0] + raw[1] + raw[2]
        places = [as_columns(pindex[k : k + 1, part]) for k in range(3)]
        amounts = [as_columns(r / total) for r in raw]
        for c in range(cown // LANES):
            value = jnp.zeros((LANES, LANES), f32)
            for k in range(3):
                value = value + jnp.where(places[k] == lanes + c * LANES, amounts[k], 0.0)
            high, low = halves(value)
            amat[part, c * LANES : (c + 1) * LANES] = high
            amat[part, cown + c * LANES : cown + (c + 1) * LANES] = low
        return carry

    def prolong_weights(part):
        lax.fori_loop(part * tiles // 4, (part + 1) * tiles // 4, prolong_block, 0, unroll=2)

    def coarse_one_hots(t, carry):
        for c in range(cper_tile // LANES):
            block = t * (cper_tile // LANES) + c
            row = coff[pl.ds(block, 1), :]
            part = span(block * LANES, LANES)
            cohg[part, :] = (as_columns(jnp.minimum(row, LANES - 1)) == lanes).astype(f32).astype(bf16)
            cohs[span(t * LANES, LANES), c * LANES : (c + 1) * LANES] = (
                (rows == row).astype(f32).astype(bf16)
            )
            origin = as_columns(crow[pl.ds(block, 1), :]) - cown
            for h in range(4 * chalo // LANES):
                cohh[part, h * LANES : (h + 1) * LANES] = (
                    (origin == lanes + h * LANES).astype(f32).astype(bf16)
                )
        return carry

    lax.fori_loop(0, cown // LANES, coarse_one_hots, 0, unroll=2)
    ctable[cown:, :] = jnp.zeros((4 * chalo, LANES), f32)
    loads[6].wait()
    prolong_weights(0)

    own = span(n * LANES, LANES)
    numer = rs_out[n]
    for d in range(1, chips):
        cross_copy(d, n, peer(N - 2 * d)).wait_recv()
        numer = numer + rs_in[chips + d]
    denom = dd_out[n]
    for d in range(1, N):
        weight_copy(d, peer(N - d)).wait_recv()
        denom = denom + dd_in[d]
    cx[own, :] = numer / (1.0 + as_columns(denom[0:1]))

    def gather_copy(slot, tile, toward):
        place = cx.at[span(tile * LANES, LANES)]
        return remote(place, place, ags.at[slot], agr.at[slot], (w, toward))

    for d in (2, 1, 3):
        gather_copy(d, n, peer(2 * d)).start()
    gather_copy(0, n, pair).start()
    prepare(2)
    prepare(3)
    prolong_weights(1)
    prolong_weights(2)
    coarse_base_edges(1)
    for d in (1, 3, 2):
        tile = peer(N - 2 * d)
        gather_copy(d, tile, tile).wait_recv()
        gather_copy(chips + d, tile, pair).start()
    prolong_weights(3)
    gather_copy(0, pair, pair).wait_recv()
    for d in (1, 3, 2):
        gather_copy(chips + d, lax.rem(pair + N - 2 * d, N), pair).wait_recv()

    cg = ga.at[pl.ds(0, cslots)]

    def coarse_copy(k, chin, chout, ss, rs, toward):
        return remote(chout.at[k], chin.at[k], ss.at[k], rs.at[k], (toward, n))

    def coarse_step(s, chin, chout, cs, cr, keep):
        take_lists(csend, cx, cpick)
        for k in range(4):
            chout[k] = mm(cpick[k], weight(s, EDGE_FROM))
        for k, dw in enumerate(COARSE_SIDES):
            @pl.when(inside(dw, 0))
            def _():
                coarse_copy(k, chin, chout, cs, cr, w + dw).start()

        wide = wide_halves(cx[...])
        ctable[0:cown, :] = fold(dot(wide, weight(s, EDGE_FROM)))
        cxc[...] = wide_halves(fold(dot(wide, weight(s, EDGE_TO))))
        cxv[...] = fold(dot(wide, weight(s, NODE_OWN)))
        if s != 1:
            coarse_base_edges(s)
        take_rows(csender, 0, cslots, ctable, cg)
        to = []
        for t in range(cown // LANES):
            here = cohg[t * cper_tile : (t + 1) * cper_tile, :]
            to.append(fold(dot(here, cxc[t * LANES : (t + 1) * LANES, :])))
        cg[...] = cg[...] + (cbase[...] + jnp.concatenate(to, axis=0))
        for k, dw in enumerate(COARSE_SIDES):
            @pl.when(inside(-dw, 0))
            def _():
                coarse_copy(k, chin, chout, cs, cr, w - dw).wait_recv()

            @pl.when(jnp.logical_not(inside(-dw, 0)))
            def _():
                chin[k] = jnp.zeros((chalo, LANES), f32)

        far = wide_halves(jnp.concatenate([chin[k] for k in range(4)], axis=0))
        h = jnp.maximum(cg[...] + fold(dot(cohh[...], far)), 0.0)
        fresh = ce[...] + normed(mm(h, weight(s, EDGE_OUT)))
        if keep:
            ce[...] = fresh
        wide = wide_halves(fresh)
        for t in range(cown // LANES):
            q = slice(t * LANES, (t + 1) * LANES)
            cagg[q, :] = fold(dot(cohs[q, :], wide[t * cper_tile : (t + 1) * cper_tile]))
        h = jnp.maximum(cxv[...] + mm(cagg[...], weight(s, NODE_SUM)), 0.0)
        fresh = cx[...] + normed(mm(h, weight(s, NODE_OUT)))
        if keep:
            for d in (2, 1, 3):
                gather_copy(d, n, peer(2 * d)).wait_send()
                gather_copy(chips + d, peer(N - 2 * d), pair).wait_send()
            gather_copy(0, n, pair).wait_send()
            cx[...] = fresh
        else:
            cfull[...] = fresh

    coarse_step(1, chin1, chout1, c1s, c1r, True)
    coarse_step(2, chin2, chout2, c2s, c2r, False)

    cstore = pltpu.make_async_copy(cfull, cout, local_sem.at[7])
    cstore.start()
    cwide = wide_halves(cfull[...])
    for b in range(nodes // 1024):
        part = slice(b * 1024, (b + 1) * 1024)
        total = dot(amat[part, 0:cown], cwide) + dot(amat[part, cown:], cwide)
        x[part, :] = x[part, :] + fold(total)

    send_halo(hout2, hin2, h2s, h2r, True)
    xstore = pltpu.make_async_copy(x, xout, local_sem.at[0])
    xstore.start()
    fine_own(3)
    xvstore = pltpu.make_async_copy(xv, xvout, local_sem.at[1])
    xvstore.start()
    wstore = pltpu.make_async_copy(wd.at[pl.ds(3 * 7 + NODE_SUM, 2)], wout, local_sem.at[2])
    wstore.start()
    fine_base(3)
    fine_halo_in(3, hout2, hin2, h2s, h2r)

    fine_edges_sums(3, False)
    store = pltpu.make_async_copy(agg, aggout, local_sem.at[3])
    store.start()

    for k in range(8):
        fine_sent(k, hout1, hin1, h1s, h1r)
        fine_sent(k, hout2, hin2, h2s, h2r)
    for d in range(1, N):
        weight_copy(d, peer(d)).wait_send()
    for i in range(chips):
        pair_copy(i, 2 * i + 1 - core).wait_send()
    for d in (2, 1, 3):
        cross_copy(d, 2 * lax.rem(chip + d, chips) + core, peer(2 * d)).wait_send()
    for k, dw in enumerate(COARSE_SIDES):
        @pl.when(inside(dw, 0))
        def _():
            coarse_copy(k, chin1, chout1, c1s, c1r, w + dw).wait_send()
            coarse_copy(k, chin2, chout2, c2s, c2r, w + dw).wait_send()
    cstore.wait()
    xstore.wait()
    xvstore.wait()
    wstore.wait()
    store.wait()


def last_nodes(x, xv, agg, weights, coarse, out, coarse_out):
    h = jnp.maximum(xv[...] + mm(agg[...], weights[0]), 0.0)
    out[...] = x[...] + normed(mm(h, weights[1]))
    coarse_out[...] = coarse[...]


def local(
    W, N,
    fine_nodes, fine_edges, fine_sender, fine_offset, fine_send,
    coarse_edges, coarse_sender, coarse_offset, coarse_send,
    restrict_source, restrict_offset, restrict_tile, restrict_weight,
    prolong_index, prolong_weight, restrict_table, prolong_table,
    edge_w1, edge_w2, node_w1, node_w2,
):
    nodes, slots = fine_nodes.shape[0], fine_edges.shape[0]
    halo, chalo = fine_send.shape[2], coarse_send.shape[2]
    tiles = nodes // LANES
    per_tile = slots // tiles
    cown = N * LANES
    cslots = coarse_edges.shape[0]
    blocks = restrict_tile.shape[0]
    smem = pl.BlockSpec(memory_space=pltpu.SMEM)
    vmem = pl.BlockSpec(memory_space=pltpu.VMEM)
    hbm = pl.BlockSpec(memory_space=pl.ANY)

    def F(*shape):
        return pltpu.VMEM(shape, f32)

    def B(*shape):
        return pltpu.VMEM(shape, bf16)

    def D(count):
        return pltpu.SemaphoreType.DMA((count,))

    row = lambda flat: flat.reshape(-1, LANES)
    parts = pl.pallas_call(
        functools.partial(kernel, (W, N)),
        out_shape=(
            jax.ShapeDtypeStruct((nodes, LANES), f32),
            jax.ShapeDtypeStruct((nodes, LANES), f32),
            jax.ShapeDtypeStruct((nodes, LANES), f32),
            jax.ShapeDtypeStruct((2, 2 * LANES, 2 * LANES), bf16),
            jax.ShapeDtypeStruct((cown, LANES), f32),
        ),
        in_specs=[smem] * 8 + [vmem] * 7 + [hbm] * 7,
        out_specs=(hbm,) * 5,
        scratch_shapes=[
            F(nodes, LANES), F(slots, LANES), F(slots, LANES), F(nodes + 8 * halo, LANES),
            B(nodes, 2 * LANES), F(nodes, LANES), F(nodes, LANES),
            F(slots, LANES),
            B(slots, LANES), B(nodes, per_tile), B(28, 2 * LANES, 2 * LANES),
            F(*edge_w1.shape), F(*edge_w2.shape), F(*node_w1.shape), F(*node_w2.shape),
            F(8, halo, LANES), F(8, halo, LANES), F(8, halo, LANES), F(8, halo, LANES),
            F(blocks, LANES), B(LANES, blocks * LANES), B(16, blocks * LANES), F(blocks * LANES, LANES),
            F(blocks, LANES, LANES), F(N, LANES, LANES), F(N, LANES, LANES),
            F(N, 8, LANES), F(N, 8, LANES),
            F(cown, LANES), F(cslots, LANES), F(cslots, LANES), F(cown + 4 * chalo, LANES),
            B(cslots, LANES), B(cown, cslots // (cown // LANES)), B(cslots, 4 * chalo),
            F(4, chalo, LANES), F(4, chalo, LANES), F(4, chalo, LANES), F(4, chalo, LANES), F(4, chalo, LANES),
            B(cown, 2 * LANES), F(cown, LANES), F(cown, LANES), F(cown, LANES),
            B(nodes, 2 * cown),
            D(8), D(8), D(8), D(8), D(8), D(N), D(N), D(N), D(N),
            D(N), D(N), D(4), D(4), D(4), D(4),
        ],
        compiler_params=pltpu.CompilerParams(
            collective_id=0, has_side_effects=True, vmem_limit_bytes=60 << 20
        ),
        name="graph_window",
    )(
        fine_sender, fine_send, coarse_sender, coarse_send, restrict_source, restrict_tile,
        restrict_table, prolong_table,
        row(fine_offset), row(coarse_offset), row(coarse_sender), row(restrict_offset), row(restrict_weight),
        prolong_index, prolong_weight,
        fine_nodes, fine_edges, coarse_edges, edge_w1, edge_w2, node_w1, node_w2,
    )
    steps = 2
    fine_rows = pl.BlockSpec((nodes // steps, LANES), lambda i: (i, 0))
    coarse_rows = pl.BlockSpec((cown // steps, LANES), lambda i: (i, 0))
    return pl.pallas_call(
        last_nodes,
        grid=(steps,),
        out_shape=(
            jax.ShapeDtypeStruct((nodes, LANES), f32),
            jax.ShapeDtypeStruct((cown, LANES), f32),
        ),
        in_specs=[fine_rows] * 3 + [vmem, coarse_rows],
        out_specs=(fine_rows, coarse_rows),
        compiler_params=pltpu.CompilerParams(vmem_limit_bytes=60 << 20),
        name="last_nodes",
    )(*parts)


def solution(mesh):
    both = ("wide", "narrow")
    placed = (
        P(both, None), P(both, None), P(both), P(both), P(both, None, None),
        P("wide", None), P("wide"), P("wide"), P("wide", None, None),
        P(both), P(both), P(both), P(both), P(None, both), P(None, both),
        P(), P(), P(), P(), P(), P(),
    )
    return jax.shard_map(
        functools.partial(local, mesh.shape["wide"], mesh.shape["narrow"]),
        mesh=mesh,
        in_specs=placed,
        out_specs=(P(both, None), P("wide", None)),
        check_vma=False,
    )
```
